256 devices in a mesh: patch: 8 (over x, core), chan: 32 (over y, z).
Axes of the slice: x: 4, y: 4, z: 8, core: 2. Of those that a mesh axis runs over, the one named last changes fastest.
Arguments:
- alpha: float32 [4096, 150], P(('patch', 'chan')), parts along dimension 0, may hold values from -0.6 to 0.6
- images: float32 [4096, 2, 128, 128], P(('patch', 'chan')), parts along dimension 0, may hold values from -6 to 6
- modes: float32 [150, 4096], replicated, may hold values from -4.8 to 4.8
- diversity: float32 [4096], replicated, may hold values from -6 to 6
- chan_of_frame: int32 [512, 1], P('chan'), may hold values from 0 to 31
Outputs:
- gradient: float32 [4096, 150], P(('patch', 'chan')), parts along dimension 0
- nb_objects: float32 [256, 2, 128, 128], P(('patch', 'chan')), parts along dimension 0
- wb_object: float32 [16, 128, 128], P('patch'), parts along dimension 0
The draws below stay inside these ranges and needn't reach their ends.
There are 8 independent parts, one for each index of `patch`. The reference program is written for one: setup_inputs(seed, part) draws one part's arguments, and reference() takes and returns one part's arrays. A program takes and returns all parts, laid end to end along the dimension named above; an argument that names none is the same for every part. Nothing has to cross between parts.
Inputs may be any that keep to these rules, and one draw needn't show every extreme that they name: `chan_of_frame`: every channel is observed in at least one frame.
All inputs are finite; a program needn't handle non-finite values.
Results may differ from the reference program's by a relative error of at most 0.0003.
Values sent between devices are 32-bit elements; how exact they have to be, the bound alone decides.
No kernel may reach another device: no remote copies, remote signals or barrier semaphores. Data moves between devices by JAX's collectives and lax.ppermute only.
A program may use at most 128 MiB of HBM per device.

```python
import math
import jax
import jax.numpy as jnp
from jax import lax

P_SIZE = 128
PUP = 64
MODES = 150
F_DEV = 16
NCH = 32
FRAMES = 512
N_CHAN = 32


def levels(stream_key, shape, shards, low, largest):
    gain = 1.0
    for dim, parts in shards:
        steps = jax.random.uniform(jax.random.fold_in(jax.random.fold_in(stream_key, 6), dim), (parts,), jnp.float32, low / len(shards), largest / len(shards))
        gain = gain * jnp.repeat(jnp.exp(steps), shape[dim] // parts).reshape((-1,) + (1,) * (len(shape) - 1 - dim))
    return gain


def picks_of(rng, rows, count, top, lift):
    ranking = jax.random.permutation(jax.random.fold_in(rng, 1), count)
    pull = ranking
    for power in range(3):
        pull = pull * pull // count
    pull = pull * lift // count
    chance = jax.random.randint(jax.random.fold_in(rng, 2), (rows, count), 0, 4096) + pull
    fixed_rows = jax.random.permutation(jax.random.fold_in(rng, 3), rows)[jnp.arange(count) % rows]
    chance = jnp.where(jnp.arange(rows)[:, None] == fixed_rows[None, :], 1 << 14, chance)
    merit = chance * count + jnp.arange(count)
    return lax.top_k(merit.astype(jnp.int32), top)[1].astype(jnp.int32)


def centred(own_key, shape, spread, limit, pieces=(), kind=jnp.bfloat16):
    factor_of = levels(own_key, shape, pieces, -0.22, 0.18) if pieces else 1.0
    array = jax.random.normal(own_key, shape, jnp.float32) * spread * factor_of
    return jnp.minimum(jnp.maximum(array, -limit), limit).astype(kind)


def setup_inputs(seed: int = 0, part: int = 0) -> dict:
    keys = jax.random.split(jax.random.key(seed), 6)
    part_keys = jax.random.split(jax.random.fold_in(keys[5], part), 6)
    alpha = centred(part_keys[0], (FRAMES, MODES), 0.1, 0.6, ((0, 32),), jnp.float32)
    images = centred(part_keys[1], (FRAMES, 2, P_SIZE, P_SIZE), 1.0, 6.0, ((0, 32),), jnp.float32)
    modes = centred(keys[2], (MODES, PUP * PUP), 0.8, 4.8, (), jnp.float32)
    diversity = centred(keys[3], (PUP * PUP,), 1.0, 6.0, (), jnp.float32)
    chan_of_frame = picks_of(keys[4], FRAMES, NCH, 1, 512)
    return dict(alpha=alpha, images=images, modes=modes, diversity=diversity, chan_of_frame=chan_of_frame)


PRECISE = lax.Precision.HIGHEST
PRIOR_WEIGHT = 0.1

def dft_table(length, columns):
    row_index = jnp.arange(length, dtype=jnp.int32)[:, None]
    col_index = jnp.arange(columns, dtype=jnp.int32)[None, :]
    angles = (row_index * col_index % length).astype(jnp.float32) * (2.0 * math.pi / length)
    return (jnp.cos(angles), -jnp.sin(angles))

def aperture(width):
    coords = jnp.arange(width, dtype=jnp.float32) - (width - 1) / 2.0
    radius = coords[:, None] ** 2 + coords[None, :] ** 2
    return (radius <= (width / 2.0) ** 2).astype(jnp.float32)

def make_tables(length, width):
    return (dft_table(length, length), dft_table(length, width), aperture(width))

def apply_left(matrix, block):
    return jnp.einsum('ux,fxy->fuy', matrix, block, precision=PRECISE)

def apply_right(block, matrix):
    return jnp.einsum('fxy,vy->fxv', block, matrix, precision=PRECISE)

def transform(table, real_part, imag_part):
    cosine, sine = table
    if imag_part is None:
        left_real = apply_left(cosine, real_part)
        left_imag = apply_left(sine, real_part)
    else:
        left_real = apply_left(cosine, real_part) - apply_left(sine, imag_part)
        left_imag = apply_left(cosine, imag_part) + apply_left(sine, real_part)
    out_real = apply_right(left_real, cosine) - apply_right(left_imag, sine)
    out_imag = apply_right(left_imag, cosine) + apply_right(left_real, sine)
    return (out_real, out_imag)

def spectra(coeffs, modes, diversity, tables):
    full_table, pupil_table, pupil = tables
    width = pupil.shape[0]
    phase = jnp.dot(coeffs, modes, precision=PRECISE).reshape(coeffs.shape[0], width, width)
    results = []
    for offset in (jnp.zeros((width, width), jnp.float32), diversity.reshape(width, width)):
        total = phase + offset
        field_real, field_imag = transform(pupil_table, pupil * jnp.cos(total), pupil * jnp.sin(total))
        power = field_real * field_real + field_imag * field_imag
        power = power / lax.optimization_barrier(jnp.sum(power, axis=(1, 2), keepdims=True))
        results.append(transform(full_table, power, None))
    return tuple(results)

def image_spectra(images_block, tables, camera):
    length = images_block.shape[-1]
    spec_real, spec_imag = transform(tables[0], images_block[:, camera], None)
    return (spec_real / length, spec_imag / length)

def frame_terms(data_pair, spec_pair):
    data_real, data_imag = data_pair
    spec_real, spec_imag = spec_pair
    return jnp.stack([data_real * spec_real + data_imag * spec_imag, data_imag * spec_real - data_real * spec_imag, spec_real * spec_real + spec_imag * spec_imag], axis=1)

def channel_onehot(chan_block, nch):
    return (chan_block[:, 0][None, :] == jnp.arange(nch, dtype=jnp.int32)[:, None]).astype(jnp.float32)

def estimate(sums):
    return sums[..., 0:2, :, :] / (PRIOR_WEIGHT + sums[..., 2:3, :, :])

def misfit(data_pair, obj_real, obj_imag, spec_pair):
    rest_real = data_pair[0] - (obj_real * spec_pair[0] - obj_imag * spec_pair[1])
    rest_imag = data_pair[1] - (obj_real * spec_pair[1] + obj_imag * spec_pair[0])
    return jnp.sum(rest_real * rest_real + rest_imag * rest_imag)

def reference(alpha, images, modes, diversity, chan_of_frame):
    tables = make_tables(P_SIZE, PUP)
    coeff_blocks = alpha.reshape(N_CHAN, F_DEV, MODES)
    image_blocks = images.reshape(N_CHAN, F_DEV, 2, P_SIZE, P_SIZE)
    chan_blocks = chan_of_frame.reshape(N_CHAN, F_DEV, 1)

    def accumulate(carry, block):
        coeffs, images_block, chan_block = block
        wide_spec, narrow_spec = spectra(coeffs, modes, diversity, tables)
        wide_terms = frame_terms(image_spectra(images_block, tables, 0), wide_spec)
        narrow_terms = frame_terms(image_spectra(images_block, tables, 1), narrow_spec)
        onehot = channel_onehot(chan_block, NCH)
        grid = jnp.einsum('kf,fcuv->kcuv', onehot, narrow_terms, precision=PRECISE)
        return ((carry[0] + lax.optimization_barrier(jnp.sum(wide_terms, axis=0)), carry[1] + grid), None)
    start = (jnp.zeros((3, P_SIZE, P_SIZE), jnp.float32), jnp.zeros((NCH, 3, P_SIZE, P_SIZE), jnp.float32))
    (wide_sums, narrow_sums), _ = lax.scan(accumulate, start, (coeff_blocks, image_blocks, chan_blocks))
    wide_object = estimate(wide_sums)
    narrow_objects = estimate(narrow_sums)

    def block_gradient(block):
        coeffs, images_block, chan_block = block
        wide_data = image_spectra(images_block, tables, 0)
        narrow_data = image_spectra(images_block, tables, 1)
        onehot = channel_onehot(chan_block, NCH)
        frame_objects = jnp.einsum('kf,kcuv->fcuv', onehot, narrow_objects, precision=PRECISE)

        def metric(values):
            wide_spec, narrow_spec = spectra(values, modes, diversity, tables)
            total = misfit(wide_data, wide_object[0], wide_object[1], wide_spec)
            total = total + misfit(narrow_data, frame_objects[:, 0], frame_objects[:, 1], narrow_spec)
            return total / (P_SIZE * P_SIZE)
        return jax.grad(metric)(coeffs)
    grads = lax.map(block_gradient, (coeff_blocks, image_blocks, chan_blocks))
    return (grads.reshape(FRAMES, MODES), narrow_objects, wide_object)
```

```python
import functools
import math

import jax
import jax.numpy as jnp
import numpy as np
from jax import lax
from jax.experimental import pallas as pl
from jax.experimental.pallas import tpu as pltpu
from jax.sharding import PartitionSpec as P

PUP = 64
SIZE = 128
HALF = SIZE // 2 + 1
ROWS = 72
NY, NZ = 4, 8
GROUP = 64 // NY
OWN = 32 // NZ
FRAMES = 16
STEP = 4
PRIOR_WEIGHT = 0.1
F32 = jnp.float32
BF16 = jnp.bfloat16
VMEM_LIMIT = 56 * 1024 * 1024
Y_ROWS = FRAMES * 3 * GROUP + FRAMES * 3
W_ROWS = 56
Z_ROWS = 216
F_ROWS = 144
R_ROWS = (FRAMES + 2) * 2 * GROUP


def dft(length, columns):
    angle = np.outer(np.arange(length), np.arange(columns)) % SIZE * (2.0 * math.pi / SIZE)
    return np.cos(angle), -np.sin(angle)


def halves(table):
    table = np.asarray(table, np.float32)
    high = table.astype(jnp.bfloat16)
    low = (table - high.astype(np.float32)).astype(jnp.bfloat16)
    return high, low


def left_short(table):
    high, low = halves(table)
    return [np.concatenate([high, high], 1), low]


def right_short(table):
    high, low = halves(table)
    return [np.concatenate([high, high], 0), low]


def make_tables():
    c, s = dft(SIZE, SIZE)
    cp, sp = dft(SIZE, PUP)
    ch, sh = np.zeros((ROWS, SIZE)), np.zeros((ROWS, SIZE))
    ch[:HALF], sh[:HALF] = c[:HALF], s[:HALF]
    weight = np.zeros((ROWS, 1))
    weight[:HALF] = 2.0
    weight[0] = weight[HALF - 1] = 1.0
    forward = (
        right_short(np.block([[cp.T, sp.T], [-sp.T, cp.T]]))
        + left_short(np.block([[cp, -sp], [sp, cp]]))
        + left_short(np.concatenate([ch, sh], 0))
        + list(halves(np.block([[c.T, s.T], [-s.T, c.T]])))
    )
    backward = (
        list(halves(np.block([[c, -s], [s, c]])))
        + list(halves(np.concatenate([(weight * ch).T, (weight * sh).T], 1)))
        + list(halves(np.block([[cp.T, sp.T], [-sp.T, cp.T]])))
        + list(halves(np.block([[cp, -sp], [sp, cp]])))
    )
    return forward, backward


def mm(a, b):
    return jnp.dot(a, b, preferred_element_type=F32)


def cut(x):
    high = x.astype(BF16)
    return high, (x - high.astype(F32)).astype(BF16)


def right_mul_short(x, twice, low):
    h, r = cut(x)
    return mm(jnp.concatenate([h, r], 1), twice[...]) + mm(h, low[...])


def left_mul_short(twice, low, x):
    h, r = cut(x)
    return mm(twice[...], jnp.concatenate([h, r], 0)) + mm(low[...], h)


def right_mul(x, high, low):
    h, r = cut(x)
    return mm(h, high[...]) + (mm(r, high[...]) + mm(h, low[...]))


def left_mul(high, low, x):
    h, r = cut(x)
    return mm(high[...], h) + (mm(high[...], r) + mm(low[...], h))


def pair_spectra(blocks, left, right):
    out = []
    for a, b in zip(blocks[::2], blocks[1::2], strict=True):
        t = left_mul_short(*left, jnp.concatenate([a, b], 1))
        for k in range(2):
            lanes = slice(k * SIZE, (k + 1) * SIZE)
            out.append(jnp.concatenate([t[:ROWS, lanes], t[ROWS:, lanes]], 1))
    full = right_mul(jnp.concatenate(out, 0), *right)
    return [full[k * ROWS : (k + 1) * ROWS] for k in range(len(blocks))]


def forward_kernel(wide, place, q_ref, im_ref, r1, r2, l1, l2, h1, h2, f1, f2, *rest):
    s_ref, d_ref, g_ref = rest[:3]
    outs, scr = rest[3 : 3 + NY], rest[3 + NY]
    step = pl.program_id(0)
    y = place[0]
    t = right_mul_short(q_ref[...].reshape(STEP * PUP, 2 * PUP), r1, r2)
    powers = []
    for a in range(0, STEP, 2):
        cols = []
        for k in (a, a + 1):
            tk = t[k * PUP : (k + 1) * PUP]
            cols.append(jnp.concatenate([tk[:, :SIZE], tk[:, SIZE:]], 0))
        g = left_mul_short(l1, l2, jnp.concatenate(cols, 1))
        for k in (a, a + 1):
            lanes = slice((k - a) * SIZE, (k - a + 1) * SIZE)
            gr, gi = g[:SIZE, lanes], g[SIZE:, lanes]
            g_ref[k, 0], g_ref[k, 1] = gr, gi
            power = gr * gr + gi * gi
            powers.append(power / jnp.sum(power, keepdims=True))
    images = [im_ref[k, 0] for k in range(STEP)]
    spectra = pair_spectra(powers + images, (h1, h2), (f1, f2))

    if wide:

        @pl.when(step == 0)
        def _():
            scr[...] = jnp.zeros_like(scr)

    for k in range(STEP):
        sk, dk = spectra[k], spectra[STEP + k] * (1.0 / SIZE)
        s_ref[k], d_ref[k] = sk, dk
        sr, si, dr, di = sk[:, :SIZE], sk[:, SIZE:], dk[:, :SIZE], dk[:, SIZE:]
        terms = (dr * sr + di * si, di * sr - dr * si, sr * sr + si * si)
        for c in range(3):
            if wide:
                scr[c] += terms[c]
            else:
                scr[c] = terms[c]
        if not wide:
            frame = step * STEP + k
            for shift in range(NY):
                row = pl.multiple_of(GROUP * lax.rem(y + shift, NY), GROUP)
                for c in range(3):
                    at = pl.multiple_of(frame * 3 * GROUP + c * GROUP, GROUP)
                    outs[shift][pl.ds(at, GROUP), :] = scr[c, pl.ds(row, GROUP), :]
                    outs[shift][pl.ds(FRAMES * 3 * GROUP + 3 * frame + c, 1), :] = scr[c, 64:65, :]

    if wide:

        @pl.when(step == FRAMES // STEP - 1)
        def _():
            for shift in range(NY):
                row = pl.multiple_of(GROUP * lax.rem(y + shift, NY), GROUP)
                for c in range(3):
                    outs[shift][c * GROUP : (c + 1) * GROUP, :] = scr[c, pl.ds(row, GROUP), :]
                    outs[shift][3 * GROUP + c : 3 * GROUP + c + 1, :] = scr[c, 64:65, :]
                outs[shift][3 * GROUP + 3 :, :] = jnp.zeros((W_ROWS - 3 * GROUP - 3, SIZE), F32)


def smem():
    return pl.BlockSpec(memory_space=pltpu.SMEM)


def whole(a):
    return pl.BlockSpec(a.shape, lambda i: (0,) * a.ndim)


def shape(*dims):
    return jax.ShapeDtypeStruct(dims, F32)


def forward(wide, place, q, images, tables):
    camera = 0 if wide else 1
    rows = W_ROWS if wide else Y_ROWS
    outs = [shape(FRAMES, ROWS, 2 * SIZE)] * 2 + [shape(FRAMES, 2, SIZE, SIZE)] + [shape(rows, SIZE)] * NY
    return pl.pallas_call(
        functools.partial(forward_kernel, wide),
        grid=(FRAMES // STEP,),
        in_specs=[
            smem(),
            pl.BlockSpec((STEP, PUP, 2 * PUP), lambda i: (i, 0, 0)),
            pl.BlockSpec((STEP, 1, SIZE, SIZE), lambda i: (i, camera, 0, 0)),
        ]
        + [whole(t) for t in tables],
        out_specs=[pl.BlockSpec((STEP, ROWS, 2 * SIZE), lambda i: (i, 0, 0))] * 2
        + [pl.BlockSpec((STEP, 2, SIZE, SIZE), lambda i: (i, 0, 0, 0))]
        + [pl.BlockSpec((rows, SIZE), lambda i: (0, 0))] * NY,
        out_shape=outs,
        scratch_shapes=[pltpu.VMEM((3, ROWS, SIZE), F32)],
        compiler_params=pltpu.CompilerParams(vmem_limit_bytes=VMEM_LIMIT),
        cost_estimate=pl.CostEstimate(flops=20_000_000_000, bytes_accessed=8_000_000, transcendentals=0),
        name="forward_wide" if wide else "forward_narrow",
    )(place, q, images, *tables)


def sum_kernel(place, ids, *refs):
    narrow, wides = refs[:NY], refs[NY : 2 * NY]
    outs = refs[2 * NY : 2 * NY + NZ]
    acc, edge, total = refs[2 * NY + NZ :]
    z = place[1]
    acc[...] = jnp.zeros_like(acc)
    edge[...] = jnp.zeros_like(edge)
    total[...] = (wides[0][...] + wides[1][...]) + (wides[2][...] + wides[3][...])
    for shift in range(NY):
        source = (NY - shift) % NY
        for f in range(FRAMES):
            k = ids[source * FRAMES + f]
            acc[k] += narrow[shift][f * 3 * GROUP : (f + 1) * 3 * GROUP, :]
            at = FRAMES * 3 * GROUP + 3 * f
            edge[k, 0:3, :] += narrow[shift][at : at + 3, :]
    for shift in range(NZ):
        to = lax.rem(z + shift, NZ)
        out = outs[shift]
        for k in range(OWN):
            out[k * 3 * GROUP : (k + 1) * 3 * GROUP, :] = acc[OWN * to + k]
            at = OWN * 3 * GROUP + 3 * k
            out[at : at + 3, :] = edge[OWN * to + k, 0:3, :]
        at = OWN * (3 * GROUP + 3)
        for c in range(3):
            for j in range(2):
                out[at + 2 * c + j : at + 2 * c + j + 1, :] = total[pl.ds(c * GROUP + 2 * to + j, 1), :]
        out[at + 6 : at + 9, :] = total[3 * GROUP : 3 * GROUP + 3, :]
        out[at + 9 :, :] = jnp.zeros((Z_ROWS - at - 9, SIZE), F32)


def quotient(num_re, num_im, den):
    den = PRIOR_WEIGHT + den
    return num_re / den, num_im / den


def object_kernel(*refs):
    parts, out = refs[:NZ], refs[NZ]
    sums = parts[0][...]
    for part in parts[1:]:
        sums = sums + part[...]
    for k in range(OWN):
        base = k * 3 * GROUP
        re, im = quotient(*(sums[base + c * GROUP : base + (c + 1) * GROUP] for c in range(3)))
        out[k * 2 * GROUP : k * 2 * GROUP + GROUP, :] = re
        out[k * 2 * GROUP + GROUP : (k + 1) * 2 * GROUP, :] = im
        base = OWN * 3 * GROUP + 3 * k
        re, im = quotient(*(sums[base + c : base + c + 1] for c in range(3)))
        at = OWN * 2 * GROUP + 2 * k
        out[at : at + 1, :] = re
        out[at + 1 : at + 2, :] = im
    base = OWN * (3 * GROUP + 3)
    at = OWN * (2 * GROUP + 2)
    re, im = quotient(*(sums[base + 2 * c : base + 2 * c + 2] for c in range(3)))
    out[at : at + 2, :] = re
    out[at + 2 : at + 4, :] = im
    re, im = quotient(*(sums[base + 6 + c : base + 7 + c] for c in range(3)))
    out[at + 4 : at + 5, :] = re
    out[at + 5 : at + 6, :] = im
    out[at + 6 :, :] = jnp.zeros((F_ROWS - at - 6, SIZE), F32)


def select_kernel(place, ids, *refs):
    parts, outs = refs[:NZ], refs[NZ : NZ + NY]
    near, objects, edge, total = refs[NZ + NY :]
    y, z = place[0], place[1]
    for shift in range(NZ):
        source = lax.rem(z + NZ - shift, NZ)
        part = parts[shift]
        for k in range(OWN):
            objects[OWN * source + k] = part[k * 2 * GROUP : (k + 1) * 2 * GROUP, :]
            at = OWN * 2 * GROUP + 2 * k
            edge[OWN * source + k, 0:2, :] = part[at : at + 2, :]
        at = OWN * (2 * GROUP + 2)
        for j in range(2):
            total[pl.ds(2 * source + j, 1), :] = part[at + j : at + j + 1, :]
            total[pl.ds(GROUP + 2 * source + j, 1), :] = part[at + 2 + j : at + 3 + j, :]
    at = OWN * (2 * GROUP + 2) + 4
    for shift in range(NY):
        out = outs[shift]
        for f in range(FRAMES):
            out[f * 2 * GROUP : (f + 1) * 2 * GROUP, :] = objects[ids[shift * FRAMES + f]]
        own = lax.rem(y + shift, NY) * NZ + z
        out[FRAMES * 2 * GROUP : (FRAMES + 1) * 2 * GROUP, :] = objects[own]
        out[(FRAMES + 1) * 2 * GROUP :, :] = total[...]
    for f in range(FRAMES):
        near[2 * f : 2 * f + 2, :] = edge[ids[f], 0:2, :]
    near[2 * FRAMES : 2 * FRAMES + 2, :] = edge[y * NZ + z, 0:2, :]
    near[2 * FRAMES + 2 : 2 * FRAMES + 4, :] = parts[0][at : at + 2, :]
    near[2 * FRAMES + 4 :, :] = jnp.zeros((4, SIZE), F32)


def plain(kernel, name, smems, arrays, outs, scratch):
    return pl.pallas_call(
        kernel,
        in_specs=[smem()] * len(smems) + [pl.BlockSpec(memory_space=pltpu.VMEM)] * len(arrays),
        out_specs=[pl.BlockSpec(memory_space=pltpu.VMEM)] * len(outs),
        out_shape=outs,
        scratch_shapes=scratch,
        compiler_params=pltpu.CompilerParams(vmem_limit_bytes=VMEM_LIMIT),
        name=name,
    )(*smems, *arrays)


def backward_kernel(wide, place, q_ref, s_ref, d_ref, g_ref, *refs):
    parts, refs = refs[:NY], refs[NY:]
    own, refs = (refs[:NY], refs[NY:]) if not wide else (None, refs)
    near, a1, a2, b1, b2, e1, e2, f1, f2, out, obj, scr = refs
    step = pl.program_id(0)
    y = place[0]

    def gather(sources, at):
        for shift in range(NY):
            row = pl.multiple_of(GROUP * lax.rem(y + NY - shift, NY), GROUP)
            for c in range(2):
                scr[c, pl.ds(row, GROUP), :] = sources[shift][at + c * GROUP : at + (c + 1) * GROUP, :]

    @pl.when(step == 0)
    def _():
        scr[...] = jnp.zeros_like(scr)
        gather(parts if wide else own, 0)
        at = 2 * FRAMES + (2 if wide else 0)
        for c in range(2):
            scr[c, 64:65, :] = near[at + c : at + c + 1, :]
        obj[...] = scr[...]

    cots = []
    for k in range(STEP):
        if not wide:
            gather(parts, k * 2 * GROUP)
            for c in range(2):
                scr[c, 64:65, :] = near[pl.ds(2 * (step * STEP + k) + c, 1), :]
        fr, fi = scr[0], scr[1]
        sk, dk = s_ref[k], d_ref[k]
        sr, si, dr, di = sk[:, :SIZE], sk[:, SIZE:], dk[:, :SIZE], dk[:, SIZE:]
        rest_r = dr - (fr * sr - fi * si)
        rest_i = di - (fr * si + fi * sr)
        cots.append(jnp.concatenate([-(rest_r * fr + rest_i * fi), rest_r * fi - rest_i * fr], 1))
    t = right_mul(jnp.concatenate(cots, 0), a1, a2)
    steps = []
    for a in range(0, STEP, 2):
        cols = []
        for k in (a, a + 1):
            tk = t[k * ROWS : (k + 1) * ROWS]
            cols.append(jnp.concatenate([tk[:, :SIZE], tk[:, SIZE:]], 0))
        dp = left_mul(b1, b2, jnp.concatenate(cols, 1))
        fields = []
        for k in (a, a + 1):
            gr, gi = g_ref[k, 0], g_ref[k, 1]
            power = gr * gr + gi * gi
            scale = 1.0 / jnp.sum(power, keepdims=True)
            dk = dp[:, (k - a) * SIZE : (k - a + 1) * SIZE]
            mean = jnp.sum(dk * power, keepdims=True) * scale
            dk = (dk - mean) * (scale * (4.0 / (SIZE * SIZE)))
            fields.append(jnp.concatenate([gr * dk, gi * dk], 0))
        h = left_mul(e1, e2, jnp.concatenate(fields, 1))
        for k in (a, a + 1):
            lanes = slice((k - a) * SIZE, (k - a + 1) * SIZE)
            steps.append(jnp.concatenate([h[:PUP, lanes], h[PUP:, lanes]], 1))
    dq = right_mul(jnp.concatenate(steps, 0), f1, f2)
    q = q_ref[...].reshape(STEP * PUP, 2 * PUP)
    dphase = q[:, :PUP] * dq[:, PUP:] - q[:, PUP:] * dq[:, :PUP]
    out[...] = dphase.reshape(STEP, PUP, PUP)


def backward(wide, place, q, s, d, g, parts, near, tables):
    item = FRAMES + 1 if wide else FRAMES
    block = 2 * GROUP
    if wide:
        sources, specs = list(parts), [pl.BlockSpec((block, SIZE), lambda i: (item, 0))] * NY
    else:
        sources = list(parts) * 2
        specs = [pl.BlockSpec((STEP * block, SIZE), lambda i: (i, 0))] * NY
        specs += [pl.BlockSpec((block, SIZE), lambda i: (item, 0))] * NY
    return pl.pallas_call(
        functools.partial(backward_kernel, wide),
        grid=(FRAMES // STEP,),
        in_specs=[
            smem(),
            pl.BlockSpec((STEP, PUP, 2 * PUP), lambda i: (i, 0, 0)),
            pl.BlockSpec((STEP, ROWS, 2 * SIZE), lambda i: (i, 0, 0)),
            pl.BlockSpec((STEP, ROWS, 2 * SIZE), lambda i: (i, 0, 0)),
            pl.BlockSpec((STEP, 2, SIZE, SIZE), lambda i: (i, 0, 0, 0)),
        ]
        + specs
        + [whole(near)]
        + [whole(t) for t in tables],
        out_specs=[
            pl.BlockSpec((STEP, PUP, PUP), lambda i: (i, 0, 0)),
            pl.BlockSpec((2, ROWS, SIZE), lambda i: (0, 0, 0)),
        ],
        out_shape=[shape(FRAMES, PUP, PUP), shape(2, ROWS, SIZE)],
        scratch_shapes=[pltpu.VMEM((2, ROWS, SIZE), F32)],
        compiler_params=pltpu.CompilerParams(vmem_limit_bytes=VMEM_LIMIT),
        cost_estimate=pl.CostEstimate(flops=20_000_000_000, bytes_accessed=8_000_000, transcendentals=0),
        name="backward_wide" if wide else "backward_narrow",
    )(place, q, s, d, g, *sources, near, *tables)


def mirrored(half):
    high = jnp.roll(jnp.flip(half[:, 1 : HALF - 1], (1, 2)), 1, 2)
    return jnp.concatenate([half[:, :HALF], high * jnp.array([1.0, -1.0], F32)[:, None, None]], 1)


def along(axis, shift):
    pairs = []
    for y in range(NY):
        for z in range(NZ):
            to = ((y + shift) % NY, z) if axis == "y" else (y, (z + shift) % NZ)
            pairs.append((y * NZ + z, to[0] * NZ + to[1]))
    return pairs


def send(x, axis, shift):
    return lax.ppermute(x, "chan", along(axis, shift))


def shards(alpha, images, modes, diversity, chan_of_frame):
    tables_f, tables_b = ([jnp.asarray(t) for t in group] for group in make_tables())
    here = lax.axis_index("chan")
    place = jnp.stack([here // NZ, here % NZ]).astype(jnp.int32)
    own_ids = chan_of_frame[:, 0]
    ids = jnp.concatenate([own_ids] + [send(own_ids, "y", -shift) for shift in range(1, NY)])

    phase = jnp.dot(alpha, modes, precision=lax.Precision.HIGHEST)
    axis = np.arange(PUP, dtype=np.float32) - (PUP - 1) / 2.0
    pupil = (axis[:, None] ** 2 + axis[None, :] ** 2 <= (PUP / 2.0) ** 2).astype(np.float32)

    def field(total):
        parts = [(jnp.asarray(pupil.reshape(-1)) * f(total)).reshape(FRAMES, PUP, PUP) for f in (jnp.cos, jnp.sin)]
        return jnp.concatenate(parts, 2)

    q_narrow = field(phase + diversity)
    q_wide = field(phase)

    narrow_s, narrow_d, narrow_g, *narrow_out = forward(False, place, q_narrow, images, tables_f)
    narrow_in = [narrow_out[0]] + [send(narrow_out[k], "y", k) for k in range(1, NY)]
    wide_s, wide_d, wide_g, *wide_out = forward(True, place, q_wide, images, tables_f)
    wide_in = [wide_out[0]] + [send(wide_out[k], "y", k) for k in range(1, NY)]

    sums = plain(
        sum_kernel,
        "sum_channels",
        [place, ids],
        narrow_in + wide_in,
        [shape(Z_ROWS, SIZE)] * NZ,
        [pltpu.VMEM((32, 3 * GROUP, SIZE), F32), pltpu.VMEM((32, 8, SIZE), F32), pltpu.VMEM((W_ROWS, SIZE), F32)],
    )
    sums = [sums[0]] + [send(sums[k], "z", k) for k in range(1, NZ)]
    (own,) = plain(object_kernel, "objects", [], sums, [shape(F_ROWS, SIZE)], [])
    every = [own] + [send(own, "z", k) for k in range(1, NZ)]
    *back, near = plain(
        select_kernel,
        "select_objects",
        [place, ids],
        every,
        [shape(R_ROWS, SIZE)] * NY + [shape(2 * FRAMES + 8, SIZE)],
        [pltpu.VMEM((32, 2 * GROUP, SIZE), F32), pltpu.VMEM((32, 8, SIZE), F32), pltpu.VMEM((2 * GROUP, SIZE), F32)],
    )
    back = [back[0]] + [send(back[k], "y", k) for k in range(1, NY)]

    wide_dphase, wide_half = backward(True, place, q_wide, wide_s, wide_d, wide_g, back, near, tables_b)
    narrow_dphase, narrow_half = backward(False, place, q_narrow, narrow_s, narrow_d, narrow_g, back, near, tables_b)
    dphase = (wide_dphase + narrow_dphase).reshape(FRAMES, PUP * PUP)
    gradient = lax.dot_general(dphase, modes, (((1,), (1,)), ((), ())), precision=lax.Precision.HIGHEST)
    return gradient, mirrored(narrow_half)[None], mirrored(wide_half)


def solution(mesh):
    placed = (
        P(("patch", "chan"), None),
        P(("patch", "chan"), None, None, None),
        P(),
        P(),
        P("chan", None),
    )
    return jax.shard_map(
        shards,
        mesh=mesh,
        in_specs=placed,
        out_specs=(
            P(("patch", "chan"), None),
            P(("patch", "chan"), None, None, None),
            P("patch", None, None),
        ),
        check_vma=False,
    )
```

```python
import functools
import math

import jax
import jax.numpy as jnp
import numpy as np
from jax import lax
from jax.experimental import pallas as pl
from jax.experimental.pallas import tpu as pltpu
from jax.sharding import PartitionSpec as P

PUP = 64
SIZE = 128
HALF = SIZE // 2 + 1
ROWS = 72
NY, NZ = 4, 8
GROUP = 64 // NY
OWN = 32 // NZ
FRAMES = 16
STEP = 16
PRIOR_WEIGHT = 0.1
F32 = jnp.float32
BF16 = jnp.bfloat16
VMEM_LIMIT = 12 * 1024 * 1024
VMEM_SMALL = 6 * 1024 * 1024
EDGES = FRAMES * 3 * GROUP
IDS = EDGES + FRAMES * 3
Y_ROWS = IDS + 8
W_ROWS = 56
ORDER = (0, 2, 1, 3)
Z_ROWS = 216
F_ROWS = 144
R_ROWS = (FRAMES + 1) * 2 * GROUP


def dft(length, columns):
    angle = np.outer(np.arange(length), np.arange(columns)) % SIZE * (2.0 * math.pi / SIZE)
    return np.cos(angle), -np.sin(angle)


def halves(table):
    table = np.asarray(table, np.float32)
    high = table.astype(jnp.bfloat16)
    low = (table - high.astype(np.float32)).astype(jnp.bfloat16)
    return high, low


def left_short(table):
    high, low = halves(table)
    return [np.concatenate([high, high], 1), low]


def right_short(table):
    high, low = halves(table)
    return [np.concatenate([high, high], 0), low]


def mirrors():
    rows, lanes = np.zeros((SIZE, SIZE)), np.zeros((SIZE, SIZE))
    for j in range(1, 64):
        rows[j, 64 - j] = 1.0
        rows[64 + j, 128 - j] = -1.0
    for v in range(SIZE):
        lanes[-v % SIZE, v] = 1.0
    return [rows.astype(jnp.bfloat16), lanes.astype(jnp.bfloat16)]


def make_tables():
    c, s = dft(SIZE, SIZE)
    cp, sp = dft(SIZE, PUP)
    order = np.r_[0:PUP:2, 1:PUP:2]
    cx, sx = cp[:, order], sp[:, order]
    ch, sh = np.zeros((ROWS, SIZE)), np.zeros((ROWS, SIZE))
    ch[:HALF], sh[:HALF] = c[:HALF], s[:HALF]
    weight = np.zeros((ROWS, 1))
    weight[:HALF] = 2.0
    weight[0] = weight[HALF - 1] = 1.0
    forward = (
        right_short(np.block([[cp.T, sp.T], [-sp.T, cp.T]]))
        + left_short(np.block([[cx, -sx], [sx, cx]]))
        + left_short(np.concatenate([ch, sh], 0))
        + list(halves(np.block([[c.T, s.T], [-s.T, c.T]])))
    )
    backward = (
        list(halves(np.block([[c, -s], [s, c]])))
        + list(halves(np.concatenate([(weight * ch).T, (weight * sh).T], 1)))
        + list(halves(np.block([[cx.T, sx.T], [-sx.T, cx.T]])))
        + list(halves(np.block([[cp, -sp], [sp, cp]])))
        + mirrors()
    )
    return forward, backward


def mm(a, b):
    return jnp.dot(a, b, preferred_element_type=F32)


def cut(x):
    high = x.astype(BF16)
    return high, (x - high.astype(F32)).astype(BF16)


def right_mul_short(x, twice, low):
    h, r = cut(x)
    return mm(jnp.concatenate([h, r], 1), twice[...]) + mm(h, low[...])


def left_mul_short(twice, low, x):
    h, r = cut(x)
    return mm(twice[...], jnp.concatenate([h, r], 0)) + mm(low[...], h)


def right_mul(x, high, low):
    h, r = cut(x)
    return mm(h, high[...]) + (mm(r, high[...]) + mm(h, low[...]))


def left_mul(high, low, x):
    h, r = cut(x)
    return mm(high[...], h) + (mm(high[...], r) + mm(low[...], h))


def pair_spectra(blocks, left, right):
    out = []
    for a, b in zip(blocks[::2], blocks[1::2], strict=True):
        t = left_mul_short(*left, jnp.concatenate([a, b], 1))
        for k in range(2):
            lanes = slice(k * SIZE, (k + 1) * SIZE)
            out.append(jnp.concatenate([t[:ROWS, lanes], t[ROWS:, lanes]], 1))
    full = right_mul(jnp.concatenate(out, 0), *right)
    return [full[k * ROWS : (k + 1) * ROWS] for k in range(len(blocks))]


def cos_sin(x):
    turns = jnp.floor(x * (2.0 / math.pi) + 0.5)
    r = ((x - turns * 1.5703125) - turns * 4.837512969970703125e-4) - turns * 7.54978995489188216e-8
    z = r * r
    sine = r + r * z * ((-1.9515295891e-4 * z + 8.3321608736e-3) * z - 1.6666654611e-1)
    cosine = 1.0 - 0.5 * z + z * z * ((2.443315711809948e-5 * z - 1.388731625493765e-3) * z + 4.166664568298827e-2)
    quarter = turns.astype(jnp.int32)
    odd = (quarter & 1) != 0
    c, s = jnp.where(odd, sine, cosine), jnp.where(odd, cosine, sine)
    return jnp.where(((quarter + 1) & 2) != 0, -c, c), jnp.where((quarter & 2) != 0, -s, s)


def low_lanes(rows):
    return lax.broadcasted_iota(jnp.int32, (rows, SIZE), 1) < PUP


def forward_kernel(wide, place, phase_ref, pupil_ref, *rest):
    if not wide:
        diversity_ref, ids_ref, *rest = rest
    im_ref, r1, r2, l1, l2, h1, h2, f1, f2, q_ref, s_ref, d_ref, g_ref, *rest = rest
    outs, scr = rest[:-1], rest[-1]
    step = pl.program_id(0)
    y = place[0]
    low = low_lanes(PUP // 2)
    for k in range(STEP):
        total = phase_ref[k]
        if not wide:
            total = total + diversity_ref[...]
        re, im = (pupil_ref[...] * part for part in cos_sin(total))
        q_ref[k, : PUP // 2, :] = jnp.where(low, re, pltpu.roll(im, PUP, 1))
        q_ref[k, PUP // 2 :, :] = jnp.where(low, pltpu.roll(re, PUP, 1), im)
    t = right_mul_short(q_ref[...].reshape(STEP * PUP, 2 * PUP), r1, r2)
    powers = []
    for a in range(0, STEP, 2):
        cols = []
        for k in (a, a + 1):
            tk = t[k * PUP : (k + 1) * PUP]
            cols.append(jnp.concatenate([tk[:, :SIZE], tk[:, SIZE:]], 0))
        g = left_mul_short(l1, l2, jnp.concatenate(cols, 1))
        for k in (a, a + 1):
            lanes = slice((k - a) * SIZE, (k - a + 1) * SIZE)
            gr, gi = g[:SIZE, lanes], g[SIZE:, lanes]
            g_ref[k, 0], g_ref[k, 1] = gr, gi
            power = gr * gr + gi * gi
            powers.append(power / jnp.sum(power, keepdims=True))
    images = [im_ref[k, 0] for k in range(STEP)]
    spectra = pair_spectra(powers + images, (h1, h2), (f1, f2))

    if wide:

        @pl.when(step == 0)
        def _():
            scr[...] = jnp.zeros_like(scr)

    for k in range(STEP):
        sk, dk = spectra[k], spectra[STEP + k] * (1.0 / SIZE)
        s_ref[k], d_ref[k] = sk, dk
        sr, si, dr, di = sk[:, :SIZE], sk[:, SIZE:], dk[:, :SIZE], dk[:, SIZE:]
        terms = (dr * sr + di * si, di * sr - dr * si, sr * sr + si * si)
        for c in range(3):
            if wide:
                scr[c] += terms[c]
            else:
                scr[c] = terms[c]
        if not wide:
            frame = step * STEP + k
            for shift in range(NY):
                row = pl.multiple_of(GROUP * lax.rem(y + shift, NY), GROUP)
                for c in range(3):
                    at = pl.multiple_of(frame * 3 * GROUP + c * GROUP, GROUP)
                    outs[shift][pl.ds(at, GROUP), :] = scr[c, pl.ds(row, GROUP), :]
                    outs[shift][pl.ds(EDGES + 3 * frame + c, 1), :] = scr[c, 64:65, :]

    @pl.when(step == 0)
    def _():
        if not wide:
            for shift in range(NY):
                outs[shift][IDS:, :] = ids_ref[...]

    if wide:

        @pl.when(step == FRAMES // STEP - 1)
        def _():
            for shift in range(NY):
                out = outs[shift // 2]
                row = pl.multiple_of(GROUP * lax.rem(y + shift, NY), GROUP)
                for c in range(3):
                    out[shift % 2, c * GROUP : (c + 1) * GROUP, :] = scr[c, pl.ds(row, GROUP), :]
                    out[shift % 2, 3 * GROUP + c : 3 * GROUP + c + 1, :] = scr[c, 64:65, :]
                out[shift % 2, 3 * GROUP + 3 :, :] = jnp.zeros((W_ROWS - 3 * GROUP - 3, SIZE), F32)


def smem():
    return pl.BlockSpec(memory_space=pltpu.SMEM)


def whole(a):
    return pl.BlockSpec(a.shape, lambda i: (0,) * a.ndim)


def shape(*dims):
    return jax.ShapeDtypeStruct(dims, F32)


def forward(wide, place, phase, pupil, extra, images, tables):
    camera = 0 if wide else 1
    outs = [shape(FRAMES, PUP, 2 * PUP)] + [shape(FRAMES, ROWS, 2 * SIZE)] * 2 + [shape(FRAMES, 2, SIZE, SIZE)]
    terms = [shape(2, W_ROWS, SIZE)] * 2 if wide else [shape(Y_ROWS, SIZE)] * NY
    return pl.pallas_call(
        functools.partial(forward_kernel, wide),
        grid=(FRAMES // STEP,),
        in_specs=[smem(), pl.BlockSpec((STEP, PUP // 2, SIZE), lambda i: (i, 0, 0)), whole(pupil)]
        + [whole(e) for e in extra]
        + [pl.BlockSpec((STEP, 1, SIZE, SIZE), lambda i: (i, camera, 0, 0))]
        + [whole(t) for t in tables],
        out_specs=[pl.BlockSpec((STEP, PUP, 2 * PUP), lambda i: (i, 0, 0))]
        + [pl.BlockSpec((STEP, ROWS, 2 * SIZE), lambda i: (i, 0, 0))] * 2
        + [pl.BlockSpec((STEP, 2, SIZE, SIZE), lambda i: (i, 0, 0, 0))]
        + [whole(t) for t in terms],
        out_shape=outs + terms,
        scratch_shapes=[pltpu.VMEM((3, ROWS, SIZE), F32)],
        compiler_params=pltpu.CompilerParams(vmem_limit_bytes=VMEM_LIMIT),
        cost_estimate=pl.CostEstimate(flops=200_000_000_000, bytes_accessed=8_000_000, transcendentals=0),
        name="forward_wide" if wide else "forward_narrow",
    )(place, phase, pupil, *extra, images, *tables)


UP, DOWN, KEEP = (1, 4, 6), (7, 2), (0, 3, 5)


def sum_kernel(place, ids, *refs):
    narrow, (w1, w2, *outs, acc, edge) = refs[:NY], refs[NY:]
    z = place[1]
    acc[...] = jnp.zeros_like(acc)
    edge[...] = jnp.zeros_like(edge)
    for source in range(NY):
        for f in range(FRAMES):
            k = ids[source * FRAMES + f]
            acc[k] += narrow[source][f * 3 * GROUP : (f + 1) * 3 * GROUP, :]
            at = EDGES + 3 * f
            edge[k, 0:3, :] += narrow[source][at : at + 3, :]
    for out, group in zip(outs, (KEEP, UP, DOWN), strict=True):
        for n, shift in enumerate(group):
            to = lax.rem(z + shift, NZ)
            start = n * Z_ROWS
            for k in range(OWN):
                at = start + k * 3 * GROUP
                out[at : at + 3 * GROUP, :] = acc[OWN * to + k]
                at = start + OWN * 3 * GROUP + 3 * k
                out[at : at + 3, :] = edge[OWN * to + k, 0:3, :]
            at = start + OWN * (3 * GROUP + 3)
            for c in range(3):
                for j in range(2):
                    row = pl.ds(GROUP * c + 2 * to + j, 1)
                    out[at + 2 * c + j : at + 2 * c + j + 1, :] = w1[row, :] + w2[row, :]
            row = slice(3 * GROUP, 3 * GROUP + 3)
            out[at + 6 : at + 9, :] = w1[row, :] + w2[row, :]
            out[at + 9 : start + Z_ROWS, :] = jnp.zeros((Z_ROWS - OWN * (3 * GROUP + 3) - 9, SIZE), F32)


def relay_kernel(keep, up, down, far, back):
    one, two = slice(Z_ROWS, 2 * Z_ROWS), slice(2 * Z_ROWS, 3 * Z_ROWS)
    far[...] = keep[one, :] + (up[one, :] + down[one, :])
    back[...] = keep[two, :] + up[two, :]


def quotient(num_re, num_im, den):
    den = PRIOR_WEIGHT + den
    return num_re / den, num_im / den


def object_kernel(keep, up, down, far, back, out):
    own = slice(0, Z_ROWS)
    sums = (keep[own, :] + (up[own, :] + down[own, :])) + (far[...] + back[...])
    for k in range(OWN):
        base = k * 3 * GROUP
        re, im = quotient(*(sums[base + c * GROUP : base + (c + 1) * GROUP] for c in range(3)))
        out[k * 2 * GROUP : k * 2 * GROUP + GROUP, :] = re
        out[k * 2 * GROUP + GROUP : (k + 1) * 2 * GROUP, :] = im
        base = OWN * 3 * GROUP + 3 * k
        re, im = quotient(*(sums[base + c : base + c + 1] for c in range(3)))
        at = OWN * 2 * GROUP + 2 * k
        out[at : at + 1, :] = re
        out[at + 1 : at + 2, :] = im
    base = OWN * (3 * GROUP + 3)
    at = OWN * (2 * GROUP + 2)
    re, im = quotient(*(sums[base + 2 * c : base + 2 * c + 2] for c in range(3)))
    out[at : at + 2, :] = re
    out[at + 2 : at + 4, :] = im
    re, im = quotient(*(sums[base + 6 + c : base + 7 + c] for c in range(3)))
    out[at + 4 : at + 5, :] = re
    out[at + 5 : at + 6, :] = im
    out[at + 6 :, :] = jnp.zeros((F_ROWS - at - 6, SIZE), F32)


def select_kernel(place, ids, own, ahead, behind, up, down, *refs):
    outs, (wide, near, objects, edge, total) = refs[:NY], refs[NY:]
    y, z = place[0], place[1]
    parts = ((0, own, 0), (3, ahead, 0), (5, behind, 0), (7, up, 0), (2, up, 1), (4, up, 2), (1, down, 0), (6, down, 1))
    for shift, part, n in parts:
        source = lax.rem(z + shift, NZ)
        start = n * F_ROWS
        for k in range(OWN):
            at = start + k * 2 * GROUP
            objects[OWN * source + k] = part[at : at + 2 * GROUP, :]
            at = start + OWN * 2 * GROUP + 2 * k
            edge[OWN * source + k, 0:2, :] = part[at : at + 2, :]
        at = start + OWN * (2 * GROUP + 2)
        for j in range(2):
            total[pl.ds(2 * source + j, 1), :] = part[at + j : at + j + 1, :]
            total[pl.ds(GROUP + 2 * source + j, 1), :] = part[at + 2 + j : at + 3 + j, :]
    wide[...] = total[...]
    for shift in range(NY):
        out = outs[shift]
        source = ORDER.index((NY - shift) % NY)
        for f in range(FRAMES):
            out[f * 2 * GROUP : (f + 1) * 2 * GROUP, :] = objects[ids[source * FRAMES + f]]
        out[FRAMES * 2 * GROUP :, :] = objects[lax.rem(y + shift, NY) * NZ + z]
    for f in range(FRAMES):
        near[2 * f : 2 * f + 2, :] = edge[ids[f], 0:2, :]
    near[2 * FRAMES : 2 * FRAMES + 2, :] = edge[y * NZ + z, 0:2, :]
    at = OWN * (2 * GROUP + 2) + 4
    near[2 * FRAMES + 2 : 2 * FRAMES + 4, :] = own[at : at + 2, :]
    near[2 * FRAMES + 4 :, :] = jnp.zeros((4, SIZE), F32)


def plain(kernel, name, smems, arrays, outs, scratch):
    return pl.pallas_call(
        kernel,
        in_specs=[smem()] * len(smems) + [pl.BlockSpec(memory_space=pltpu.VMEM)] * len(arrays),
        out_specs=[pl.BlockSpec(memory_space=pltpu.VMEM)] * len(outs),
        out_shape=outs,
        scratch_shapes=scratch,
        compiler_params=pltpu.CompilerParams(vmem_limit_bytes=VMEM_SMALL),
        name=name,
    )(*smems, *arrays)


def backward_kernel(wide, place, q_ref, s_ref, d_ref, g_ref, *refs):
    parts, refs = refs[:NY], refs[NY:]
    if not wide:
        own, (other, *refs) = refs[:NY], refs[NY:]
    near, a1, a2, b1, b2, e1, e2, f1, f2, m1, m2, out, obj, scr = refs
    step = pl.program_id(0)
    y = place[0]

    def gather(sources, at):
        for shift in range(NY):
            row = pl.multiple_of(GROUP * lax.rem(y + NY - shift, NY), GROUP)
            for c in range(2):
                scr[c, pl.ds(row, GROUP), :] = sources[shift][at + c * GROUP : at + (c + 1) * GROUP, :]

    @pl.when(step == 0)
    def _():
        scr[...] = jnp.zeros_like(scr)
        gather(parts if wide else own, 0)
        at = 2 * FRAMES + (2 if wide else 0)
        for c in range(2):
            scr[c, 64:65, :] = near[at + c : at + c + 1, :]
        half = jnp.concatenate([scr[0, :64, :], scr[1, :64, :]], 0)
        high = half.astype(BF16)
        middle, low = cut(half - high.astype(F32))
        turned = jnp.zeros((SIZE, SIZE), F32)
        for part in (high, middle, low):
            turned = turned + mm(m1[...], mm(part, m2[...]).astype(BF16))
        for c in range(2):
            obj[c, :64, :] = scr[c, :64, :]
            obj[c, 64:, :] = turned[64 * c : 64 * (c + 1)]
            obj[c, 64:65, :] = scr[c, 64:65, :]

    cots = []
    for k in range(STEP):
        if not wide:
            gather(parts, k * 2 * GROUP)
            for c in range(2):
                scr[c, 64:65, :] = near[pl.ds(2 * (step * STEP + k) + c, 1), :]
        fr, fi = scr[0], scr[1]
        sk, dk = s_ref[k], d_ref[k]
        sr, si, dr, di = sk[:, :SIZE], sk[:, SIZE:], dk[:, :SIZE], dk[:, SIZE:]
        rest_r = dr - (fr * sr - fi * si)
        rest_i = di - (fr * si + fi * sr)
        cots.append(jnp.concatenate([-(rest_r * fr + rest_i * fi), rest_r * fi - rest_i * fr], 1))
    t = right_mul(jnp.concatenate(cots, 0), a1, a2)
    steps = []
    for a in range(0, STEP, 2):
        cols = []
        for k in (a, a + 1):
            tk = t[k * ROWS : (k + 1) * ROWS]
            cols.append(jnp.concatenate([tk[:, :SIZE], tk[:, SIZE:]], 0))
        dp = left_mul(b1, b2, jnp.concatenate(cols, 1))
        fields = []
        for k in (a, a + 1):
            gr, gi = g_ref[k, 0], g_ref[k, 1]
            power = gr * gr + gi * gi
            scale = 1.0 / jnp.sum(power, keepdims=True)
            dk = dp[:, (k - a) * SIZE : (k - a + 1) * SIZE]
            mean = jnp.sum(dk * power, keepdims=True) * scale
            dk = (dk - mean) * (scale * (4.0 / (SIZE * SIZE)))
            fields.append(jnp.concatenate([gr * dk, gi * dk], 0))
        h = left_mul(e1, e2, jnp.concatenate(fields, 1))
        for k in (a, a + 1):
            lanes = slice((k - a) * SIZE, (k - a + 1) * SIZE)
            steps.append(jnp.concatenate([h[:PUP, lanes], h[PUP:, lanes]], 1))
    dq = right_mul(jnp.concatenate(steps, 0), f1, f2)
    low = low_lanes(PUP // 2)
    flat = []
    for k in range(STEP):
        m = q_ref[k] * pltpu.roll(dq[k * PUP : (k + 1) * PUP], PUP, 1)
        m = m - pltpu.roll(m, PUP, 1)
        dphase = jnp.where(low, m[: PUP // 2], -m[PUP // 2 :])
        if wide:
            out[k] = dphase
        else:
            flat.append(dphase + other[k])
    for at in range(0, FRAMES if flat else 0, STEP):

        @pl.when(step * STEP == at)
        def _(at=at):
            for k, dphase in enumerate(flat):
                for r in range(PUP // 2):
                    out[at + k : at + k + 1, r * SIZE : (r + 1) * SIZE] = dphase[r : r + 1]


def backward(wide, place, q, s, d, g, parts, near, other, tables):
    block = 2 * GROUP
    pairs = pl.BlockSpec((STEP, PUP // 2, SIZE), lambda i: (i, 0, 0))
    if wide:
        sources, specs = list(parts), [whole(p) for p in parts]
        dphase, dphase_spec = shape(FRAMES, PUP // 2, SIZE), pairs
    else:
        sources = list(parts) * 2 + [other]
        specs = [pl.BlockSpec((STEP * block, SIZE), lambda i: (i, 0))] * NY
        specs += [pl.BlockSpec((block, SIZE), lambda i: (FRAMES, 0))] * NY + [pairs]
        dphase = shape(FRAMES, PUP * PUP)
        dphase_spec = pl.BlockSpec(dphase.shape, lambda i: (0, 0))
    return pl.pallas_call(
        functools.partial(backward_kernel, wide),
        grid=(FRAMES // STEP,),
        in_specs=[
            smem(),
            pl.BlockSpec((STEP, PUP, 2 * PUP), lambda i: (i, 0, 0)),
            pl.BlockSpec((STEP, ROWS, 2 * SIZE), lambda i: (i, 0, 0)),
            pl.BlockSpec((STEP, ROWS, 2 * SIZE), lambda i: (i, 0, 0)),
            pl.BlockSpec((STEP, 2, SIZE, SIZE), lambda i: (i, 0, 0, 0)),
        ]
        + specs
        + [whole(near)]
        + [whole(t) for t in tables],
        out_specs=[dphase_spec, pl.BlockSpec((2, SIZE, SIZE), lambda i: (0, 0, 0))],
        out_shape=[dphase, shape(2, SIZE, SIZE)],
        scratch_shapes=[pltpu.VMEM((2, ROWS, SIZE), F32)],
        compiler_params=pltpu.CompilerParams(vmem_limit_bytes=VMEM_LIMIT),
        cost_estimate=pl.CostEstimate(flops=200_000_000_000, bytes_accessed=8_000_000, transcendentals=0),
        name="backward_wide" if wide else "backward_narrow",
    )(place, q, s, d, g, *sources, near, *tables)


def along(axis, shift):
    pairs = []
    for y in range(NY):
        for z in range(NZ):
            to = ((y + shift) % NY, z) if axis == "y" else (y, (z + shift) % NZ)
            pairs.append((y * NZ + z, to[0] * NZ + to[1]))
    return pairs


def send(x, axis, shift):
    return lax.ppermute(x, "chan", along(axis, shift))


def shards(alpha, images, modes, diversity, chan_of_frame):
    tables_f, tables_b = ([jnp.asarray(t) for t in group] for group in make_tables())
    here = lax.axis_index("chan")
    place = jnp.stack([here // NZ, here % NZ]).astype(jnp.int32)
    own_ids = jnp.zeros((8, SIZE), F32).at[0, :FRAMES].set(chan_of_frame[:, 0].astype(F32))

    phase = jnp.dot(alpha, modes, precision=lax.Precision.HIGH).reshape(FRAMES, PUP // 2, SIZE)
    axis = np.arange(PUP, dtype=np.float32) - (PUP - 1) / 2.0
    pupil = (axis[:, None] ** 2 + axis[None, :] ** 2 <= (PUP / 2.0) ** 2).astype(np.float32)
    pupil = jnp.asarray(pupil.reshape(PUP // 2, SIZE))
    extra = [diversity.reshape(PUP // 2, SIZE), own_ids]

    *narrow_kept, n0, n1, n2, n3 = forward(False, place, phase, pupil, extra, images, tables_f)
    narrow_in = [n0] + [send((n0, n1, n2, n3)[k], "y", k) for k in ORDER[1:]]
    *wide_kept, near, far = forward(True, place, phase, pupil, [], images, tables_f)
    near = near + send(far, "y", 2)
    wide_in = [near[0], send(near[1], "y", 1)]
    ids = jnp.concatenate([part[IDS, :FRAMES] for part in narrow_in]).astype(jnp.int32)

    keep, up, down = plain(
        sum_kernel,
        "sum_channels",
        [place, ids],
        narrow_in + wide_in,
        [shape(len(group) * Z_ROWS, SIZE) for group in (KEEP, UP, DOWN)],
        [pltpu.VMEM((32, 3 * GROUP, SIZE), F32), pltpu.VMEM((32, 8, SIZE), F32)],
    )
    up, down = send(up, "z", 1), send(down, "z", -1)
    far, back = plain(relay_kernel, "relay", [], [keep, up, down], [shape(Z_ROWS, SIZE)] * 2, [])
    far, back = send(far, "z", 3), send(back, "z", -3)
    (own,) = plain(object_kernel, "objects", [], [keep, up, down, far, back], [shape(F_ROWS, SIZE)], [])
    ahead, behind = send(own, "z", -3), send(own, "z", 3)
    up = send(jnp.concatenate([own, ahead, behind]), "z", 1)
    down = send(jnp.concatenate([own, behind]), "z", -1)
    *back, wide_own, near = plain(
        select_kernel,
        "select_objects",
        [place, ids],
        [own, ahead, behind, up, down],
        [shape(R_ROWS, SIZE)] * NY + [shape(2 * GROUP, SIZE), shape(2 * FRAMES + 8, SIZE)],
        [pltpu.VMEM((32, 2 * GROUP, SIZE), F32), pltpu.VMEM((32, 8, SIZE), F32), pltpu.VMEM((2 * GROUP, SIZE), F32)],
    )
    wide_back = [wide_own] + [send(wide_own, "y", k) for k in range(1, NY)]
    back = [back[0]] + [send(back[k], "y", k) for k in range(1, NY)]

    wide_dphase, wide_object = backward(True, place, *wide_kept, wide_back, near, None, tables_b)
    dphase, narrow_object = backward(False, place, *narrow_kept, back, near, wide_dphase, tables_b)
    gradient = lax.dot_general(dphase, modes, (((1,), (1,)), ((), ())), precision=lax.Precision.HIGH)
    return gradient, narrow_object[None], wide_object


def solution(mesh):
    placed = (
        P(("patch", "chan"), None),
        P(("patch", "chan"), None, None, None),
        P(),
        P(),
        P("chan", None),
    )
    return jax.shard_map(
        shards,
        mesh=mesh,
        in_specs=placed,
        out_specs=(
            P(("patch", "chan"), None),
            P(("patch", "chan"), None, None, None),
            P("patch", None, None),
        ),
        check_vma=False,
    )
```

```python
import functools
import math

import jax
import jax.numpy as jnp
import numpy as np
from jax import lax
from jax.experimental import pallas as pl
from jax.experimental.pallas import tpu as pltpu
from jax.sharding import PartitionSpec as P

PUP = 64
SIZE = 128
HALF = SIZE // 2 + 1
ROWS = 72
NY, NZ = 4, 8
GROUP = 64 // NY
OWN = 32 // NZ
FRAMES = 16
STEP = 16
PRIOR_WEIGHT = 0.1
F32 = jnp.float32
BF16 = jnp.bfloat16
VMEM_LIMIT = 8 * 1024 * 1024
VMEM_SMALL = 4 * 1024 * 1024
EDGES = FRAMES * 3 * GROUP
IDS = EDGES + FRAMES * 3
Y_ROWS = IDS + 8
W_ROWS = 56
BASE = (0, W_ROWS, 0, W_ROWS)
Z_ROWS = 216
F_ROWS = 144
R_ROWS = (FRAMES + 1) * 2 * GROUP


def dft(length, columns):
    angle = np.outer(np.arange(length), np.arange(columns)) % SIZE * (2.0 * math.pi / SIZE)
    return np.cos(angle), -np.sin(angle)


def halves(table):
    table = np.asarray(table, np.float32)
    high = table.astype(jnp.bfloat16)
    low = (table - high.astype(np.float32)).astype(jnp.bfloat16)
    return high, low


def left_short(table):
    high, low = halves(table)
    return [np.concatenate([high, high], 1), low]


def right_short(table):
    high, low = halves(table)
    return [np.concatenate([high, high], 0), low]


def mirrors():
    rows, lanes = np.zeros((SIZE, SIZE)), np.zeros((SIZE, SIZE))
    for j in range(1, 64):
        rows[j, 64 - j] = 1.0
        rows[64 + j, 128 - j] = -1.0
    for v in range(SIZE):
        lanes[-v % SIZE, v] = 1.0
    return [rows.astype(jnp.bfloat16), lanes.astype(jnp.bfloat16)]


def make_tables():
    c, s = dft(SIZE, SIZE)
    cp, sp = dft(SIZE, PUP)
    order = np.r_[0:PUP:2, 1:PUP:2]
    cx, sx = cp[:, order], sp[:, order]
    ch, sh = np.zeros((ROWS, SIZE)), np.zeros((ROWS, SIZE))
    ch[:HALF], sh[:HALF] = c[:HALF], s[:HALF]
    weight = np.zeros((ROWS, 1))
    weight[:HALF] = 2.0
    weight[0] = weight[HALF - 1] = 1.0
    forward = (
        right_short(np.block([[cp.T, sp.T], [-sp.T, cp.T]]))
        + left_short(np.block([[cx, -sx], [sx, cx]]))
        + left_short(np.concatenate([ch, sh], 0))
        + list(halves(np.block([[c.T, s.T], [-s.T, c.T]])))
    )
    backward = (
        list(halves(np.block([[c, -s], [s, c]])))
        + list(halves(np.concatenate([(weight * ch).T, (weight * sh).T], 1)))
        + list(halves(np.block([[cx.T, sx.T], [-sx.T, cx.T]])))
        + list(halves(np.block([[cp, -sp], [sp, cp]])))
        + mirrors()
    )
    return forward, backward


def mm(a, b):
    return jnp.dot(a, b, preferred_element_type=F32)


def cut(x):
    high = x.astype(BF16)
    return high, (x - high.astype(F32)).astype(BF16)


def right_mul_short(x, twice, low):
    h, r = cut(x)
    return mm(jnp.concatenate([h, r], 1), twice[...]) + mm(h, low[...])


def left_mul_short(twice, low, x):
    h, r = cut(x)
    return mm(twice[...], jnp.concatenate([h, r], 0)) + mm(low[...], h)


def right_mul(x, high, low):
    h, r = cut(x)
    return mm(h, high[...]) + (mm(r, high[...]) + mm(h, low[...]))


def left_mul(high, low, x):
    h, r = cut(x)
    return mm(high[...], h) + (mm(high[...], r) + mm(low[...], h))


def pair_spectra(blocks, left, right):
    out = []
    for a, b in zip(blocks[::2], blocks[1::2], strict=True):
        t = left_mul_short(*left, jnp.concatenate([a, b], 1))
        for k in range(2):
            lanes = slice(k * SIZE, (k + 1) * SIZE)
            out.append(jnp.concatenate([t[:ROWS, lanes], t[ROWS:, lanes]], 1))
    full = right_mul(jnp.concatenate(out, 0), *right)
    return [full[k * ROWS : (k + 1) * ROWS] for k in range(len(blocks))]


def cos_sin(x):
    turns = jnp.floor(x * (2.0 / math.pi) + 0.5)
    r = ((x - turns * 1.5703125) - turns * 4.837512969970703125e-4) - turns * 7.54978995489188216e-8
    z = r * r
    sine = r + r * z * ((-1.9515295891e-4 * z + 8.3321608736e-3) * z - 1.6666654611e-1)
    cosine = 1.0 - 0.5 * z + z * z * ((2.443315711809948e-5 * z - 1.388731625493765e-3) * z + 4.166664568298827e-2)
    quarter = turns.astype(jnp.int32)
    odd = (quarter & 1) != 0
    c, s = jnp.where(odd, sine, cosine), jnp.where(odd, cosine, sine)
    return jnp.where(((quarter + 1) & 2) != 0, -c, c), jnp.where((quarter & 2) != 0, -s, s)


def low_lanes(rows):
    return lax.broadcasted_iota(jnp.int32, (rows, SIZE), 1) < PUP


def forward_kernel(wide, place, phase_ref, pupil_ref, *rest):
    if not wide:
        diversity_ref, ids_ref, *rest = rest
    else:
        _, _, *rest = rest
    im_ref, r1, r2, l1, l2, h1, h2, f1, f2, q_ref, s_ref, d_ref, g_ref, *outs, scr = rest
    step = pl.program_id(0)
    y = place[0]
    low = low_lanes(PUP // 2)
    for k in range(STEP):
        total = phase_ref[k]
        if not wide:
            total = total + diversity_ref[...]
        re, im = (pupil_ref[...] * part for part in cos_sin(total))
        q_ref[k, : PUP // 2, :] = jnp.where(low, re, pltpu.roll(im, PUP, 1))
        q_ref[k, PUP // 2 :, :] = jnp.where(low, pltpu.roll(re, PUP, 1), im)
    t = right_mul_short(q_ref[...].reshape(STEP * PUP, 2 * PUP), r1, r2)
    powers = []
    for a in range(0, STEP, 2):
        cols = []
        for k in (a, a + 1):
            tk = t[k * PUP : (k + 1) * PUP]
            cols.append(jnp.concatenate([tk[:, :SIZE], tk[:, SIZE:]], 0))
        g = left_mul_short(l1, l2, jnp.concatenate(cols, 1))
        for k in (a, a + 1):
            lanes = slice((k - a) * SIZE, (k - a + 1) * SIZE)
            gr, gi = g[:SIZE, lanes], g[SIZE:, lanes]
            g_ref[k, 0], g_ref[k, 1] = gr, gi
            power = gr * gr + gi * gi
            powers.append(power * (1.0 / jnp.sum(power, keepdims=True)))
    images = [im_ref[k, 0] for k in range(STEP)]
    spectra = pair_spectra(powers + images, (h1, h2), (f1, f2))

    if wide:

        @pl.when(step == 0)
        def _():
            scr[...] = jnp.zeros_like(scr)

    for k in range(STEP):
        sk, dk = spectra[k], spectra[STEP + k] * (1.0 / SIZE)
        s_ref[k], d_ref[k] = sk, dk
        sr, si, dr, di = sk[:, :SIZE], sk[:, SIZE:], dk[:, :SIZE], dk[:, SIZE:]
        terms = (dr * sr + di * si, di * sr - dr * si, sr * sr + si * si)
        for c in range(3):
            if wide:
                scr[c] += terms[c]
            else:
                scr[c] = terms[c]
        if not wide:
            frame = step * STEP + k
            for shift in range(NY):
                row = pl.multiple_of(GROUP * lax.rem(y + shift, NY), GROUP)
                for c in range(3):
                    at = pl.multiple_of(BASE[shift] + frame * 3 * GROUP + c * GROUP, 8)
                    outs[shift][pl.ds(at, GROUP), :] = scr[c, pl.ds(row, GROUP), :]
                    outs[shift][pl.ds(BASE[shift] + EDGES + 3 * frame + c, 1), :] = scr[c, 64:65, :]

    @pl.when(step == 0)
    def _():
        if not wide:
            for shift in range(NY):
                outs[shift][BASE[shift] + IDS :, :] = ids_ref[...]

    if wide:

        @pl.when(step == FRAMES // STEP - 1)
        def _():
            for shift in range(NY):
                out = outs[shift]
                row = pl.multiple_of(GROUP * lax.rem(y + shift, NY), GROUP)
                for c in range(3):
                    out[c * GROUP : (c + 1) * GROUP, :] = scr[c, pl.ds(row, GROUP), :]
                    out[3 * GROUP + c : 3 * GROUP + c + 1, :] = scr[c, 64:65, :]
                out[3 * GROUP + 3 :, :] = jnp.zeros((W_ROWS - 3 * GROUP - 3, SIZE), F32)


def smem():
    return pl.BlockSpec(memory_space=pltpu.SMEM)


def whole(a):
    return pl.BlockSpec(a.shape, lambda i: (0,) * a.ndim)


def shape(*dims):
    return jax.ShapeDtypeStruct(dims, F32)


def forward(wide, place, phase, pupil, extra, images, tables):
    camera = 0 if wide else 1
    outs = [shape(FRAMES, PUP, 2 * PUP)] + [shape(FRAMES, ROWS, 2 * SIZE)] * 2 + [shape(FRAMES, 2, SIZE, SIZE)]
    terms = [shape(W_ROWS if wide and not base else Y_ROWS + base, SIZE) for base in BASE]
    return pl.pallas_call(
        functools.partial(forward_kernel, wide),
        grid=(FRAMES // STEP,),
        in_specs=[smem(), pl.BlockSpec((STEP, PUP // 2, SIZE), lambda i: (i, 0, 0)), whole(pupil)]
        + [pl.BlockSpec(memory_space=pl.ANY) if wide else whole(e) for e in extra]
        + [pl.BlockSpec((STEP, 1, SIZE, SIZE), lambda i: (i, camera, 0, 0))]
        + [whole(t) for t in tables],
        out_specs=[pl.BlockSpec((STEP, PUP, 2 * PUP), lambda i: (i, 0, 0))]
        + [pl.BlockSpec((STEP, ROWS, 2 * SIZE), lambda i: (i, 0, 0))] * 2
        + [pl.BlockSpec((STEP, 2, SIZE, SIZE), lambda i: (i, 0, 0, 0))]
        + [pl.BlockSpec((W_ROWS, SIZE), lambda i: (0, 0)) if wide else whole(t) for t in terms],
        out_shape=outs + terms,
        input_output_aliases={3: len(outs) + 1, 4: len(outs) + 3} if wide else {},
        scratch_shapes=[pltpu.VMEM((3, ROWS, SIZE), F32)],
        compiler_params=pltpu.CompilerParams(vmem_limit_bytes=VMEM_LIMIT),
        cost_estimate=pl.CostEstimate(flops=200_000_000_000, bytes_accessed=8_000_000, transcendentals=0),
        name="forward_wide" if wide else "forward_narrow",
    )(place, phase, pupil, *extra, images, *tables)


UP, DOWN, KEEP = (1, 6, 4), (7, 2, 4), (0, 3, 5)
Z_FIRST, F_FIRST = 112, 72
UP_ROWS, DOWN_ROWS = 2 * Z_ROWS + Z_FIRST, 3 * Z_ROWS - Z_FIRST


def number_copies(sources, bases, numbers, arrived):
    return [
        pltpu.make_async_copy(source.at[pl.ds(base + IDS, 8)], numbers.at[n], arrived.at[n])
        for n, (source, base) in enumerate(zip(sources, bases, strict=True))
    ]


def add_frames(sources, bases, acc, edge, numbers):
    for n, (source, base) in enumerate(zip(sources, bases, strict=True)):
        for f in range(FRAMES):
            k = numbers[n, 0, f].astype(jnp.int32)
            at = base + f * 3 * GROUP
            acc[k] += source[at : at + 3 * GROUP, :]
            at = base + EDGES + 3 * f
            edge[k, 0:3, :] += source[at : at + 3, :]


def first_sum_kernel(n0, n2, acc, edge, numbers, arrived):
    copies = number_copies((n0, n2), (BASE[0], BASE[2]), numbers, arrived)
    for copy in copies:
        copy.start()
    acc[...] = jnp.zeros_like(acc)
    edge[...] = jnp.zeros_like(edge)
    for copy in copies:
        copy.wait()
    add_frames((n0, n2), (BASE[0], BASE[2]), acc, edge, numbers)


def sum_kernel(place, first, first_edge, n1, n3, w0, w2, keep, up, down, acc, edge, block, total, numbers, arrived):
    z = place[1]
    copies = number_copies((n1, n3), (BASE[1], BASE[3]), numbers, arrived)
    for copy in copies:
        copy.start()
    acc[...] = first[...]
    edge[...] = first_edge[...]
    total[...] = (w0[...] + w2[...]) + (n1[:W_ROWS, :] + n3[:W_ROWS, :])
    for copy in copies:
        copy.wait()
    add_frames((n1, n3), (BASE[1], BASE[3]), acc, edge, numbers)

    def pack(out, group):
        for n, shift in enumerate(group):
            to = lax.rem(z + shift, NZ)
            start = n * Z_ROWS
            for k in range(OWN):
                at = start + k * 3 * GROUP
                out[at : at + 3 * GROUP, :] = acc[OWN * to + k]
                at = start + OWN * 3 * GROUP + 3 * k
                out[at : at + 3, :] = edge[OWN * to + k, 0:3, :]
            at = start + OWN * (3 * GROUP + 3)
            for c in range(3):
                for j in range(2):
                    row = pl.ds(GROUP * c + 2 * to + j, 1)
                    out[at + 2 * c + j : at + 2 * c + j + 1, :] = total[row, :]
            row = slice(3 * GROUP, 3 * GROUP + 3)
            out[at + 6 : at + 9, :] = total[row, :]
            out[at + 9 : start + Z_ROWS, :] = jnp.zeros((Z_ROWS - OWN * (3 * GROUP + 3) - 9, SIZE), F32)

    pack(keep, KEEP)
    pack(up, UP[:2])
    pack(down, DOWN[:2])
    pack(block, UP[2:])
    up[2 * Z_ROWS :, :] = block[:Z_FIRST, :]
    down[2 * Z_ROWS :, :] = block[Z_FIRST:, :]


def relay_kernel(keep, up, down, far, back):
    end = 2 * Z_ROWS
    far[:Z_FIRST, :] = keep[Z_ROWS : Z_ROWS + Z_FIRST, :] + (up[end:, :] + down[Z_ROWS : Z_ROWS + Z_FIRST, :])
    far[Z_FIRST:, :] = keep[Z_ROWS + Z_FIRST : end, :] + down[Z_ROWS + Z_FIRST : end, :]
    back[:Z_FIRST, :] = keep[end : end + Z_FIRST, :] + up[Z_ROWS : Z_ROWS + Z_FIRST, :]
    back[Z_FIRST:, :] = keep[end + Z_FIRST :, :] + (up[Z_ROWS + Z_FIRST : end, :] + down[end:, :])


def quotient(num_re, num_im, den):
    den = PRIOR_WEIGHT + den
    return num_re / den, num_im / den


def object_kernel(keep, up, down, far, back, out):
    own = slice(0, Z_ROWS)
    sums = (keep[own, :] + (up[own, :] + down[own, :])) + (far[...] + back[...])
    for k in range(OWN):
        base = k * 3 * GROUP
        re, im = quotient(*(sums[base + c * GROUP : base + (c + 1) * GROUP] for c in range(3)))
        out[k * 2 * GROUP : k * 2 * GROUP + GROUP, :] = re
        out[k * 2 * GROUP + GROUP : (k + 1) * 2 * GROUP, :] = im
        base = OWN * 3 * GROUP + 3 * k
        re, im = quotient(*(sums[base + c : base + c + 1] for c in range(3)))
        at = OWN * 2 * GROUP + 2 * k
        out[at : at + 1, :] = re
        out[at + 1 : at + 2, :] = im
    base = OWN * (3 * GROUP + 3)
    at = OWN * (2 * GROUP + 2)
    re, im = quotient(*(sums[base + 2 * c : base + 2 * c + 2] for c in range(3)))
    out[at : at + 2, :] = re
    out[at + 2 : at + 4, :] = im
    re, im = quotient(*(sums[base + 6 + c : base + 7 + c] for c in range(3)))
    out[at + 4 : at + 5, :] = re
    out[at + 5 : at + 6, :] = im
    out[at + 6 :, :] = jnp.zeros((F_ROWS - at - 6, SIZE), F32)


def select_kernel(place, ids, own, ahead, behind, up, down, *refs):
    outs, (wide, near, objects, edge, total, other) = refs[:NY], refs[NY:]
    other[:F_FIRST, :] = up[2 * F_ROWS :, :]
    other[F_FIRST:, :] = down[2 * F_ROWS :, :]
    y, z = place[0], place[1]
    parts = ((0, own, 0), (3, ahead, 0), (5, behind, 0), (7, up, 0), (2, up, 1), (1, down, 0), (6, down, 1), (4, other, 0))
    for shift, part, n in parts:
        source = lax.rem(z + shift, NZ)
        start = n * F_ROWS
        for k in range(OWN):
            at = start + k * 2 * GROUP
            objects[OWN * source + k] = part[at : at + 2 * GROUP, :]
            at = start + OWN * 2 * GROUP + 2 * k
            edge[OWN * source + k, 0:2, :] = part[at : at + 2, :]
        at = start + OWN * (2 * GROUP + 2)
        for j in range(2):
            total[pl.ds(2 * source + j, 1), :] = part[at + j : at + j + 1, :]
            total[pl.ds(GROUP + 2 * source + j, 1), :] = part[at + 2 + j : at + 3 + j, :]
    wide[...] = total[...]
    for shift in range(NY):
        out = outs[shift]
        start = (NY - shift) % NY * FRAMES
        for f in range(FRAMES):
            out[f * 2 * GROUP : (f + 1) * 2 * GROUP, :] = objects[ids[start + f]]
        out[FRAMES * 2 * GROUP :, :] = objects[lax.rem(y + shift, NY) * NZ + z]
    for f in range(FRAMES):
        near[2 * f : 2 * f + 2, :] = edge[ids[f], 0:2, :]
    near[2 * FRAMES : 2 * FRAMES + 2, :] = edge[y * NZ + z, 0:2, :]
    at = OWN * (2 * GROUP + 2) + 4
    near[2 * FRAMES + 2 : 2 * FRAMES + 4, :] = own[at : at + 2, :]
    near[2 * FRAMES + 4 :, :] = jnp.zeros((4, SIZE), F32)


def plain(kernel, name, smems, arrays, outs, scratch, cost=None):
    return pl.pallas_call(
        kernel,
        in_specs=[smem()] * len(smems) + [pl.BlockSpec(memory_space=pltpu.VMEM)] * len(arrays),
        out_specs=[pl.BlockSpec(memory_space=pltpu.VMEM)] * len(outs),
        out_shape=outs,
        scratch_shapes=scratch,
        compiler_params=pltpu.CompilerParams(vmem_limit_bytes=VMEM_SMALL),
        cost_estimate=cost,
        name=name,
    )(*smems, *arrays)


def backward_kernel(wide, place, q_ref, s_ref, d_ref, g_ref, *refs):
    parts, refs = refs[:NY], refs[NY:]
    if not wide:
        own, (other, *refs) = refs[:NY], refs[NY:]
    near, a1, a2, b1, b2, e1, e2, f1, f2, m1, m2, out, obj, scr = refs
    step = pl.program_id(0)
    y = place[0]

    def gather(sources, at):
        for shift in range(NY):
            row = pl.multiple_of(GROUP * lax.rem(y + NY - shift, NY), GROUP)
            for c in range(2):
                scr[c, pl.ds(row, GROUP), :] = sources[shift][at + c * GROUP : at + (c + 1) * GROUP, :]

    @pl.when(step == 0)
    def _():
        scr[...] = jnp.zeros_like(scr)
        gather(parts if wide else own, 0)
        at = 2 * FRAMES + (2 if wide else 0)
        for c in range(2):
            scr[c, 64:65, :] = near[at + c : at + c + 1, :]
        half = jnp.concatenate([scr[0, :64, :], scr[1, :64, :]], 0)
        high = half.astype(BF16)
        middle, low = cut(half - high.astype(F32))
        turned = jnp.zeros((SIZE, SIZE), F32)
        for part in (high, middle, low):
            turned = turned + mm(m1[...], mm(part, m2[...]).astype(BF16))
        for c in range(2):
            obj[c, :64, :] = scr[c, :64, :]
            obj[c, 64:, :] = turned[64 * c : 64 * (c + 1)]
            obj[c, 64:65, :] = scr[c, 64:65, :]

    cots = []
    for k in range(STEP):
        if not wide:
            gather(parts, k * 2 * GROUP)
            for c in range(2):
                scr[c, 64:65, :] = near[pl.ds(2 * (step * STEP + k) + c, 1), :]
        fr, fi = scr[0], scr[1]
        sk, dk = s_ref[k], d_ref[k]
        sr, si, dr, di = sk[:, :SIZE], sk[:, SIZE:], dk[:, :SIZE], dk[:, SIZE:]
        rest_r = dr - (fr * sr - fi * si)
        rest_i = di - (fr * si + fi * sr)
        cots.append(jnp.concatenate([-(rest_r * fr + rest_i * fi), rest_r * fi - rest_i * fr], 1))
    t = right_mul(jnp.concatenate(cots, 0), a1, a2)
    steps = []
    for a in range(0, STEP, 2):
        cols = []
        for k in (a, a + 1):
            tk = t[k * ROWS : (k + 1) * ROWS]
            cols.append(jnp.concatenate([tk[:, :SIZE], tk[:, SIZE:]], 0))
        dp = left_mul(b1, b2, jnp.concatenate(cols, 1))
        fields = []
        for k in (a, a + 1):
            gr, gi = g_ref[k, 0], g_ref[k, 1]
            power = gr * gr + gi * gi
            scale = 1.0 / jnp.sum(power, keepdims=True)
            dk = dp[:, (k - a) * SIZE : (k - a + 1) * SIZE]
            mean = jnp.sum(dk * power, keepdims=True) * scale
            dk = (dk - mean) * (scale * (4.0 / (SIZE * SIZE)))
            fields.append(jnp.concatenate([gr * dk, gi * dk], 0))
        h = left_mul(e1, e2, jnp.concatenate(fields, 1))
        for k in (a, a + 1):
            lanes = slice((k - a) * SIZE, (k - a + 1) * SIZE)
            steps.append(jnp.concatenate([h[:PUP, lanes], h[PUP:, lanes]], 1))
    dq = right_mul(jnp.concatenate(steps, 0), f1, f2)
    low = low_lanes(PUP // 2)
    flat = []
    for k in range(STEP):
        m = q_ref[k] * pltpu.roll(dq[k * PUP : (k + 1) * PUP], PUP, 1)
        m = m - pltpu.roll(m, PUP, 1)
        dphase = jnp.where(low, m[: PUP // 2], -m[PUP // 2 :])
        if wide:
            out[k] = dphase
        else:
            flat.append(dphase + other[k])
    for at in range(0, FRAMES if flat else 0, STEP):

        @pl.when(step * STEP == at)
        def _(at=at):
            for k, dphase in enumerate(flat):
                for r in range(PUP // 2):
                    out[at + k : at + k + 1, r * SIZE : (r + 1) * SIZE] = dphase[r : r + 1]


def backward(wide, place, q, s, d, g, parts, near, other, tables):
    block = 2 * GROUP
    pairs = pl.BlockSpec((STEP, PUP // 2, SIZE), lambda i: (i, 0, 0))
    if wide:
        sources, specs = list(parts), [whole(p) for p in parts]
        dphase, dphase_spec = shape(FRAMES, PUP // 2, SIZE), pairs
    else:
        sources = list(parts) * 2 + [other]
        specs = [pl.BlockSpec((STEP * block, SIZE), lambda i: (i, 0))] * NY
        specs += [pl.BlockSpec((block, SIZE), lambda i: (FRAMES, 0))] * NY + [pairs]
        dphase = shape(FRAMES, PUP * PUP)
        dphase_spec = pl.BlockSpec(dphase.shape, lambda i: (0, 0))
    return pl.pallas_call(
        functools.partial(backward_kernel, wide),
        grid=(FRAMES // STEP,),
        in_specs=[
            smem(),
            pl.BlockSpec((STEP, PUP, 2 * PUP), lambda i: (i, 0, 0)),
            pl.BlockSpec((STEP, ROWS, 2 * SIZE), lambda i: (i, 0, 0)),
            pl.BlockSpec((STEP, ROWS, 2 * SIZE), lambda i: (i, 0, 0)),
            pl.BlockSpec((STEP, 2, SIZE, SIZE), lambda i: (i, 0, 0, 0)),
        ]
        + specs
        + [whole(near)]
        + [whole(t) for t in tables],
        out_specs=[dphase_spec, pl.BlockSpec((2, SIZE, SIZE), lambda i: (0, 0, 0))],
        out_shape=[dphase, shape(2, SIZE, SIZE)],
        scratch_shapes=[pltpu.VMEM((2, ROWS, SIZE), F32)],
        compiler_params=pltpu.CompilerParams(vmem_limit_bytes=VMEM_LIMIT),
        cost_estimate=pl.CostEstimate(flops=200_000_000_000, bytes_accessed=8_000_000, transcendentals=0),
        name="backward_wide" if wide else "backward_narrow",
    )(place, q, s, d, g, *sources, near, *tables)


def along(axis, shift):
    pairs = []
    for y in range(NY):
        for z in range(NZ):
            to = ((y + shift) % NY, z) if axis == "y" else (y, (z + shift) % NZ)
            pairs.append((y * NZ + z, to[0] * NZ + to[1]))
    return pairs


def send(x, axis, shift):
    return lax.ppermute(x, "chan", along(axis, shift))


def shards(alpha, images, modes, diversity, chan_of_frame):
    tables_f, tables_b = ([jnp.asarray(t) for t in group] for group in make_tables())
    here = lax.axis_index("chan")
    place = jnp.stack([here // NZ, here % NZ]).astype(jnp.int32)
    own_ids = jnp.zeros((8, SIZE), F32).at[0, :FRAMES].set(chan_of_frame[:, 0].astype(F32))

    phase = jnp.dot(alpha, modes, precision=lax.Precision.HIGH).reshape(FRAMES, PUP // 2, SIZE)
    axis = np.arange(PUP, dtype=np.float32) - (PUP - 1) / 2.0
    pupil = (axis[:, None] ** 2 + axis[None, :] ** 2 <= (PUP / 2.0) ** 2).astype(np.float32)
    pupil = jnp.asarray(pupil.reshape(PUP // 2, SIZE))
    extra = [diversity.reshape(PUP // 2, SIZE), own_ids]

    *narrow_kept, n0, n1, n2, n3 = forward(False, place, phase, pupil, extra, images, tables_f)
    *wide_kept, w0, n1, w2, n3 = forward(True, place, phase, pupil, [n1, n3], images, tables_f)
    n2 = send(n2, "y", 2)
    reading = [pltpu.SMEM((2, 8, SIZE), F32), pltpu.SemaphoreType.DMA((2,))]
    first, first_edge = plain(
        first_sum_kernel,
        "sum_first",
        [],
        [n0, n2],
        [shape(32, 3 * GROUP, SIZE), shape(32, 8, SIZE)],
        reading,
        pl.CostEstimate(flops=200_000_000_000, bytes_accessed=2_000_000, transcendentals=0),
    )
    n1, n3 = send(n1, "y", 1), send(n3, "y", 3)
    keep, up, down = plain(
        sum_kernel,
        "sum_channels",
        [place],
        [first, first_edge, n1, n3, w0, send(w2, "y", 2)],
        [shape(rows, SIZE) for rows in (3 * Z_ROWS, UP_ROWS, DOWN_ROWS)],
        [
            pltpu.VMEM((32, 3 * GROUP, SIZE), F32),
            pltpu.VMEM((32, 8, SIZE), F32),
            pltpu.VMEM((Z_ROWS, SIZE), F32),
            pltpu.VMEM((W_ROWS, SIZE), F32),
            *reading,
        ],
    )
    ids = jnp.concatenate([n[base + IDS, :FRAMES] for n, base in zip((n0, n1, n2, n3), BASE, strict=True)])
    ids = ids.astype(jnp.int32)
    up, down = send(up, "z", 1), send(down, "z", -1)
    far, back = plain(relay_kernel, "relay", [], [keep, up, down], [shape(Z_ROWS, SIZE)] * 2, [])
    far, back = send(far, "z", 3), send(back, "z", -3)
    (own,) = plain(object_kernel, "objects", [], [keep, up, down, far, back], [shape(F_ROWS, SIZE)], [])
    ahead, behind = send(own, "z", -3), send(own, "z", 3)
    up = send(jnp.concatenate([own, ahead, behind[:F_FIRST]]), "z", 1)
    down = send(jnp.concatenate([own, behind, ahead[F_FIRST:]]), "z", -1)
    *back, wide_own, near = plain(
        select_kernel,
        "select_objects",
        [place, ids],
        [own, ahead, behind, up, down],
        [shape(R_ROWS, SIZE)] * NY + [shape(2 * GROUP, SIZE), shape(2 * FRAMES + 8, SIZE)],
        [pltpu.VMEM((32, 2 * GROUP, SIZE), F32), pltpu.VMEM((32, 8, SIZE), F32), pltpu.VMEM((2 * GROUP, SIZE), F32), pltpu.VMEM((F_ROWS, SIZE), F32)],
    )
    wide_back = [wide_own] + [send(wide_own, "y", k) for k in range(1, NY)]
    back = [back[0]] + [send(back[k], "y", k) for k in range(1, NY)]

    wide_dphase, wide_object = backward(True, place, *wide_kept, wide_back, near, None, tables_b)
    dphase, narrow_object = backward(False, place, *narrow_kept, back, near, wide_dphase, tables_b)
    gradient = lax.dot_general(dphase, modes, (((1,), (1,)), ((), ())), precision=lax.Precision.HIGH)
    return gradient, narrow_object[None], wide_object


def solution(mesh):
    placed = (
        P(("patch", "chan"), None),
        P(("patch", "chan"), None, None, None),
        P(),
        P(),
        P("chan", None),
    )
    return jax.shard_map(
        shards,
        mesh=mesh,
        in_specs=placed,
        out_specs=(
            P(("patch", "chan"), None),
            P(("patch", "chan"), None, None, None),
            P("patch", None, None),
        ),
        check_vma=False,
    )
```

```python
import functools
import math

import jax
import jax.numpy as jnp
import numpy as np
from jax import lax
from jax.experimental import pallas as pl
from jax.experimental.pallas import tpu as pltpu
from jax.sharding import PartitionSpec as P

PUP = 64
SIZE = 128
HALF = SIZE // 2 + 1
ROWS = 72
NY, NZ = 4, 8
GROUP = 64 // NY
OWN = 32 // NZ
FRAMES = 16
STEP = 16
PRIOR_WEIGHT = 0.1
F32 = jnp.float32
BF16 = jnp.bfloat16
VMEM_LIMIT = 8 * 1024 * 1024
VMEM_SMALL = 4 * 1024 * 1024
EDGES = FRAMES * 3 * GROUP
IDS = EDGES + FRAMES * 3
Y_ROWS = IDS + 8
W_ROWS = 56
BASE = (0, W_ROWS, 0, W_ROWS)
Z_ROWS = 216
F_ROWS = 144
R_ROWS = (FRAMES + 1) * 2 * GROUP


def dft(length, columns):
    angle = np.outer(np.arange(length), np.arange(columns)) % SIZE * (2.0 * math.pi / SIZE)
    return np.cos(angle), -np.sin(angle)


def halves(table):
    table = np.asarray(table, np.float32)
    high = table.astype(jnp.bfloat16)
    low = (table - high.astype(np.float32)).astype(jnp.bfloat16)
    return high, low


def left_short(table):
    high, low = halves(table)
    return [np.concatenate([high, high], 1), low]


def right_short(table):
    high, low = halves(table)
    return [np.concatenate([high, high], 0), low]


def mirrors():
    rows, lanes = np.zeros((SIZE, SIZE)), np.zeros((SIZE, SIZE))
    for j in range(1, 64):
        rows[j, 64 - j] = 1.0
        rows[64 + j, 128 - j] = -1.0
    for v in range(SIZE):
        lanes[-v % SIZE, v] = 1.0
    return [rows.astype(jnp.bfloat16), lanes.astype(jnp.bfloat16)]


def make_tables():
    c, s = dft(SIZE, SIZE)
    cp, sp = dft(SIZE, PUP)
    order = np.r_[0:PUP:2, 1:PUP:2]
    cx, sx = cp[:, order], sp[:, order]
    ch, sh = np.zeros((ROWS, SIZE)), np.zeros((ROWS, SIZE))
    ch[:HALF], sh[:HALF] = c[:HALF], s[:HALF]
    weight = np.zeros((ROWS, 1))
    weight[:HALF] = 2.0
    weight[0] = weight[HALF - 1] = 1.0
    forward = (
        right_short(np.block([[cp.T, sp.T], [-sp.T, cp.T]]))
        + left_short(np.block([[cx, -sx], [sx, cx]]))
        + left_short(np.concatenate([ch, sh], 0))
        + list(halves(np.block([[c.T, s.T], [-s.T, c.T]])))
    )
    backward = (
        list(halves(np.block([[c, -s], [s, c]])))
        + list(halves(np.concatenate([(weight * ch).T, (weight * sh).T], 1)))
        + list(halves(np.block([[cx.T, sx.T], [-sx.T, cx.T]])))
        + list(halves(np.block([[cp, -sp], [sp, cp]])))
        + mirrors()
    )
    return forward, backward


def mm(a, b):
    return jnp.dot(a, b, preferred_element_type=F32)


def cut(x):
    high = x.astype(BF16)
    return high, (x - high.astype(F32)).astype(BF16)


def right_mul_short(x, twice, low):
    h, r = cut(x)
    return mm(jnp.concatenate([h, r], 1), twice[...]) + mm(h, low[...])


def left_mul_short(twice, low, x):
    h, r = cut(x)
    return mm(twice[...], jnp.concatenate([h, r], 0)) + mm(low[...], h)


def right_mul(x, high, low):
    h, r = cut(x)
    return mm(h, high[...]) + (mm(r, high[...]) + mm(h, low[...]))


def left_mul(high, low, x):
    h, r = cut(x)
    return mm(high[...], h) + (mm(high[...], r) + mm(low[...], h))


def pair_spectra(blocks, left, right):
    out = []
    for a, b in zip(blocks[::2], blocks[1::2], strict=True):
        t = left_mul_short(*left, jnp.concatenate([a, b], 1))
        for k in range(2):
            lanes = slice(k * SIZE, (k + 1) * SIZE)
            out.append(jnp.concatenate([t[:ROWS, lanes], t[ROWS:, lanes]], 1))
    full = right_mul(jnp.concatenate(out, 0), *right)
    return [full[k * ROWS : (k + 1) * ROWS] for k in range(len(blocks))]


def cos_sin(x):
    turns = jnp.floor(x * (2.0 / math.pi) + 0.5)
    r = ((x - turns * 1.5703125) - turns * 4.837512969970703125e-4) - turns * 7.54978995489188216e-8
    z = r * r
    sine = r + r * z * ((-1.9515295891e-4 * z + 8.3321608736e-3) * z - 1.6666654611e-1)
    cosine = 1.0 - 0.5 * z + z * z * ((2.443315711809948e-5 * z - 1.388731625493765e-3) * z + 4.166664568298827e-2)
    quarter = turns.astype(jnp.int32)
    odd = (quarter & 1) != 0
    c, s = jnp.where(odd, sine, cosine), jnp.where(odd, cosine, sine)
    return jnp.where(((quarter + 1) & 2) != 0, -c, c), jnp.where((quarter & 2) != 0, -s, s)


def low_lanes(rows):
    return lax.broadcasted_iota(jnp.int32, (rows, SIZE), 1) < PUP


def forward_kernel(wide, place, phase_ref, pupil_ref, *rest):
    if not wide:
        diversity_ref, ids_ref, *rest = rest
    else:
        _, _, *rest = rest
    im_ref, r1, r2, l1, l2, h1, h2, f1, f2, q_ref, s_ref, d_ref, g_ref, *outs, scr = rest
    step = pl.program_id(0)
    y = place[0]
    low = low_lanes(PUP // 2)
    for k in range(STEP):
        total = phase_ref[k]
        if not wide:
            total = total + diversity_ref[...]
        re, im = (pupil_ref[...] * part for part in cos_sin(total))
        q_ref[k, : PUP // 2, :] = jnp.where(low, re, pltpu.roll(im, PUP, 1))
        q_ref[k, PUP // 2 :, :] = jnp.where(low, pltpu.roll(re, PUP, 1), im)
    t = right_mul_short(q_ref[...].reshape(STEP * PUP, 2 * PUP), r1, r2)
    powers = []
    for a in range(0, STEP, 2):
        cols = []
        for k in (a, a + 1):
            tk = t[k * PUP : (k + 1) * PUP]
            cols.append(jnp.concatenate([tk[:, :SIZE], tk[:, SIZE:]], 0))
        g = left_mul_short(l1, l2, jnp.concatenate(cols, 1))
        for k in (a, a + 1):
            lanes = slice((k - a) * SIZE, (k - a + 1) * SIZE)
            gr, gi = g[:SIZE, lanes], g[SIZE:, lanes]
            g_ref[k, 0], g_ref[k, 1] = gr, gi
            power = gr * gr + gi * gi
            powers.append(power * (1.0 / jnp.sum(power, keepdims=True)))
    images = [im_ref[k, 0] for k in range(STEP)]
    spectra = pair_spectra(powers + images, (h1, h2), (f1, f2))

    if wide:

        @pl.when(step == 0)
        def _():
            scr[...] = jnp.zeros_like(scr)

    for k in range(STEP):
        sk, dk = spectra[k], spectra[STEP + k] * (1.0 / SIZE)
        s_ref[k], d_ref[k] = sk, dk
        sr, si, dr, di = sk[:, :SIZE], sk[:, SIZE:], dk[:, :SIZE], dk[:, SIZE:]
        terms = (dr * sr + di * si, di * sr - dr * si, sr * sr + si * si)
        for c in range(3):
            if wide:
                scr[c] += terms[c]
            else:
                scr[c] = terms[c]
        if not wide:
            frame = step * STEP + k
            for shift in range(NY):
                row = pl.multiple_of(GROUP * lax.rem(y + shift, NY), GROUP)
                for c in range(3):
                    at = pl.multiple_of(BASE[shift] + frame * 3 * GROUP + c * GROUP, 8)
                    outs[shift][pl.ds(at, GROUP), :] = scr[c, pl.ds(row, GROUP), :]
                    outs[shift][pl.ds(BASE[shift] + EDGES + 3 * frame + c, 1), :] = scr[c, 64:65, :]

    @pl.when(step == 0)
    def _():
        if not wide:
            for shift in range(NY):
                outs[shift][BASE[shift] + IDS :, :] = ids_ref[...]

    if wide:

        @pl.when(step == FRAMES // STEP - 1)
        def _():
            for shift in range(NY):
                out = outs[shift]
                row = pl.multiple_of(GROUP * lax.rem(y + shift, NY), GROUP)
                for c in range(3):
                    out[c * GROUP : (c + 1) * GROUP, :] = scr[c, pl.ds(row, GROUP), :]
                    out[3 * GROUP + c : 3 * GROUP + c + 1, :] = scr[c, 64:65, :]
                out[3 * GROUP + 3 :, :] = jnp.zeros((W_ROWS - 3 * GROUP - 3, SIZE), F32)


def smem():
    return pl.BlockSpec(memory_space=pltpu.SMEM)


def whole(a):
    return pl.BlockSpec(a.shape, lambda i: (0,) * a.ndim)


def shape(*dims):
    return jax.ShapeDtypeStruct(dims, F32)


def forward(wide, place, phase, pupil, extra, images, tables):
    camera = 0 if wide else 1
    outs = [shape(FRAMES, PUP, 2 * PUP)] + [shape(FRAMES, ROWS, 2 * SIZE)] * 2 + [shape(FRAMES, 2, SIZE, SIZE)]
    terms = [shape(W_ROWS if wide and not base else Y_ROWS + base, SIZE) for base in BASE]
    return pl.pallas_call(
        functools.partial(forward_kernel, wide),
        grid=(FRAMES // STEP,),
        in_specs=[smem(), pl.BlockSpec((STEP, PUP // 2, SIZE), lambda i: (i, 0, 0)), whole(pupil)]
        + [pl.BlockSpec(memory_space=pl.ANY) if wide else whole(e) for e in extra]
        + [pl.BlockSpec((STEP, 1, SIZE, SIZE), lambda i: (i, camera, 0, 0))]
        + [whole(t) for t in tables],
        out_specs=[pl.BlockSpec((STEP, PUP, 2 * PUP), lambda i: (i, 0, 0))]
        + [pl.BlockSpec((STEP, ROWS, 2 * SIZE), lambda i: (i, 0, 0))] * 2
        + [pl.BlockSpec((STEP, 2, SIZE, SIZE), lambda i: (i, 0, 0, 0))]
        + [pl.BlockSpec((W_ROWS, SIZE), lambda i: (0, 0)) if wide else whole(t) for t in terms],
        out_shape=outs + terms,
        input_output_aliases={3: len(outs) + 1, 4: len(outs) + 3} if wide else {},
        scratch_shapes=[pltpu.VMEM((3, ROWS, SIZE), F32)],
        compiler_params=pltpu.CompilerParams(vmem_limit_bytes=VMEM_LIMIT),
        cost_estimate=pl.CostEstimate(flops=4_000_000_000, bytes_accessed=8_000_000, transcendentals=0),
        name="forward_wide" if wide else "forward_narrow",
    )(place, phase, pupil, *extra, images, *tables)


UP, DOWN, KEEP = (1, 6, 4), (7, 2, 4), (0, 3, 5)
Z_FIRST, F_FIRST = 112, 72
UP_ROWS, DOWN_ROWS = 2 * Z_ROWS + Z_FIRST, 3 * Z_ROWS - Z_FIRST


def number_copies(sources, bases, numbers, arrived):
    return [
        pltpu.make_async_copy(source.at[pl.ds(base + IDS, 8)], numbers.at[n], arrived.at[n])
        for n, (source, base) in enumerate(zip(sources, bases, strict=True))
    ]


def add_frames(sources, bases, acc, edge, numbers):
    for n, (source, base) in enumerate(zip(sources, bases, strict=True)):
        for f in range(FRAMES):
            k = numbers[n, 0, f].astype(jnp.int32)
            at = base + f * 3 * GROUP
            acc[k] += source[at : at + 3 * GROUP, :]
            at = base + EDGES + 3 * f
            edge[k, 0:3, :] += source[at : at + 3, :]


def first_sum_kernel(n0, n2, acc, edge, numbers, arrived):
    copies = number_copies((n0, n2), (BASE[0], BASE[2]), numbers, arrived)
    for copy in copies:
        copy.start()
    acc[...] = jnp.zeros_like(acc)
    edge[...] = jnp.zeros_like(edge)
    for copy in copies:
        copy.wait()
    add_frames((n0, n2), (BASE[0], BASE[2]), acc, edge, numbers)


def sum_kernel(place, first, first_edge, n1, n3, w0, w2, keep, up, down, acc, edge, block, total, numbers, arrived):
    z = place[1]
    copies = number_copies((n1, n3), (BASE[1], BASE[3]), numbers, arrived)
    for copy in copies:
        copy.start()
    acc[...] = first[...]
    edge[...] = first_edge[...]
    total[...] = (w0[...] + w2[...]) + (n1[:W_ROWS, :] + n3[:W_ROWS, :])
    for copy in copies:
        copy.wait()
    add_frames((n1, n3), (BASE[1], BASE[3]), acc, edge, numbers)

    def pack(out, group):
        for n, shift in enumerate(group):
            to = lax.rem(z + shift, NZ)
            start = n * Z_ROWS
            for k in range(OWN):
                at = start + k * 3 * GROUP
                out[at : at + 3 * GROUP, :] = acc[OWN * to + k]
                at = start + OWN * 3 * GROUP + 3 * k
                out[at : at + 3, :] = edge[OWN * to + k, 0:3, :]
            at = start + OWN * (3 * GROUP + 3)
            for c in range(3):
                for j in range(2):
                    row = pl.ds(GROUP * c + 2 * to + j, 1)
                    out[at + 2 * c + j : at + 2 * c + j + 1, :] = total[row, :]
            row = slice(3 * GROUP, 3 * GROUP + 3)
            out[at + 6 : at + 9, :] = total[row, :]
            out[at + 9 : start + Z_ROWS, :] = jnp.zeros((Z_ROWS - OWN * (3 * GROUP + 3) - 9, SIZE), F32)

    pack(keep, KEEP)
    pack(up, UP[:2])
    pack(down, DOWN[:2])
    pack(block, UP[2:])
    up[2 * Z_ROWS :, :] = block[:Z_FIRST, :]
    down[2 * Z_ROWS :, :] = block[Z_FIRST:, :]


def relay_kernel(keep, up, down, far, back):
    end = 2 * Z_ROWS
    far[:Z_FIRST, :] = keep[Z_ROWS : Z_ROWS + Z_FIRST, :] + (up[end:, :] + down[Z_ROWS : Z_ROWS + Z_FIRST, :])
    far[Z_FIRST:, :] = keep[Z_ROWS + Z_FIRST : end, :] + down[Z_ROWS + Z_FIRST : end, :]
    back[:Z_FIRST, :] = keep[end : end + Z_FIRST, :] + up[Z_ROWS : Z_ROWS + Z_FIRST, :]
    back[Z_FIRST:, :] = keep[end + Z_FIRST :, :] + (up[Z_ROWS + Z_FIRST : end, :] + down[end:, :])


def quotient(num_re, num_im, den):
    den = PRIOR_WEIGHT + den
    return num_re / den, num_im / den


def object_kernel(keep, up, down, far, back, out):
    own = slice(0, Z_ROWS)
    sums = (keep[own, :] + (up[own, :] + down[own, :])) + (far[...] + back[...])
    for k in range(OWN):
        base = k * 3 * GROUP
        re, im = quotient(*(sums[base + c * GROUP : base + (c + 1) * GROUP] for c in range(3)))
        out[k * 2 * GROUP : k * 2 * GROUP + GROUP, :] = re
        out[k * 2 * GROUP + GROUP : (k + 1) * 2 * GROUP, :] = im
        base = OWN * 3 * GROUP + 3 * k
        re, im = quotient(*(sums[base + c : base + c + 1] for c in range(3)))
        at = OWN * 2 * GROUP + 2 * k
        out[at : at + 1, :] = re
        out[at + 1 : at + 2, :] = im
    base = OWN * (3 * GROUP + 3)
    at = OWN * (2 * GROUP + 2)
    re, im = quotient(*(sums[base + 2 * c : base + 2 * c + 2] for c in range(3)))
    out[at : at + 2, :] = re
    out[at + 2 : at + 4, :] = im
    re, im = quotient(*(sums[base + 6 + c : base + 7 + c] for c in range(3)))
    out[at + 4 : at + 5, :] = re
    out[at + 5 : at + 6, :] = im
    out[at + 6 :, :] = jnp.zeros((F_ROWS - at - 6, SIZE), F32)


def select_kernel(place, ids, own, ahead, behind, up, down, *refs):
    outs, (wide, near, objects, edge, total, other) = refs[:NY], refs[NY:]
    other[:F_FIRST, :] = up[2 * F_ROWS :, :]
    other[F_FIRST:, :] = down[2 * F_ROWS :, :]
    y, z = place[0], place[1]
    parts = ((0, own, 0), (3, ahead, 0), (5, behind, 0), (7, up, 0), (2, up, 1), (1, down, 0), (6, down, 1), (4, other, 0))
    for shift, part, n in parts:
        source = lax.rem(z + shift, NZ)
        start = n * F_ROWS
        for k in range(OWN):
            at = start + k * 2 * GROUP
            objects[OWN * source + k] = part[at : at + 2 * GROUP, :]
            at = start + OWN * 2 * GROUP + 2 * k
            edge[OWN * source + k, 0:2, :] = part[at : at + 2, :]
        at = start + OWN * (2 * GROUP + 2)
        for j in range(2):
            total[pl.ds(2 * source + j, 1), :] = part[at + j : at + j + 1, :]
            total[pl.ds(GROUP + 2 * source + j, 1), :] = part[at + 2 + j : at + 3 + j, :]
    wide[...] = total[...]
    for shift in range(NY):
        out = outs[shift]
        start = (NY - shift) % NY * FRAMES
        for f in range(FRAMES):
            out[f * 2 * GROUP : (f + 1) * 2 * GROUP, :] = objects[ids[start + f]]
        out[FRAMES * 2 * GROUP :, :] = objects[lax.rem(y + shift, NY) * NZ + z]
    for f in range(FRAMES):
        near[2 * f : 2 * f + 2, :] = edge[ids[f], 0:2, :]
    near[2 * FRAMES : 2 * FRAMES + 2, :] = edge[y * NZ + z, 0:2, :]
    at = OWN * (2 * GROUP + 2) + 4
    near[2 * FRAMES + 2 : 2 * FRAMES + 4, :] = own[at : at + 2, :]
    near[2 * FRAMES + 4 :, :] = jnp.zeros((4, SIZE), F32)


def plain(kernel, name, smems, arrays, outs, scratch, cost=None):
    return pl.pallas_call(
        kernel,
        in_specs=[smem()] * len(smems) + [pl.BlockSpec(memory_space=pltpu.VMEM)] * len(arrays),
        out_specs=[pl.BlockSpec(memory_space=pltpu.VMEM)] * len(outs),
        out_shape=outs,
        scratch_shapes=scratch,
        compiler_params=pltpu.CompilerParams(vmem_limit_bytes=VMEM_SMALL),
        cost_estimate=cost,
        name=name,
    )(*smems, *arrays)


def backward_kernel(wide, place, q_ref, s_ref, d_ref, g_ref, *refs):
    parts, refs = refs[:NY], refs[NY:]
    if not wide:
        own, (other, *refs) = refs[:NY], refs[NY:]
    near, a1, a2, b1, b2, e1, e2, f1, f2, m1, m2, out, obj, scr = refs
    step = pl.program_id(0)
    y = place[0]

    def gather(sources, at):
        for shift in range(NY):
            row = pl.multiple_of(GROUP * lax.rem(y + NY - shift, NY), GROUP)
            for c in range(2):
                scr[c, pl.ds(row, GROUP), :] = sources[shift][at + c * GROUP : at + (c + 1) * GROUP, :]

    @pl.when(step == 0)
    def _():
        scr[...] = jnp.zeros_like(scr)
        gather(parts if wide else own, 0)
        at = 2 * FRAMES + (2 if wide else 0)
        for c in range(2):
            scr[c, 64:65, :] = near[at + c : at + c + 1, :]
        half = jnp.concatenate([scr[0, :64, :], scr[1, :64, :]], 0)
        high = half.astype(BF16)
        middle, low = cut(half - high.astype(F32))
        turned = jnp.zeros((SIZE, SIZE), F32)
        for part in (high, middle, low):
            turned = turned + mm(m1[...], mm(part, m2[...]).astype(BF16))
        for c in range(2):
            obj[c, :64, :] = scr[c, :64, :]
            obj[c, 64:, :] = turned[64 * c : 64 * (c + 1)]
            obj[c, 64:65, :] = scr[c, 64:65, :]

    cots = []
    for k in range(STEP):
        if not wide:
            gather(parts, k * 2 * GROUP)
            for c in range(2):
                scr[c, 64:65, :] = near[pl.ds(2 * (step * STEP + k) + c, 1), :]
        fr, fi = scr[0], scr[1]
        sk, dk = s_ref[k], d_ref[k]
        sr, si, dr, di = sk[:, :SIZE], sk[:, SIZE:], dk[:, :SIZE], dk[:, SIZE:]
        rest_r = dr - (fr * sr - fi * si)
        rest_i = di - (fr * si + fi * sr)
        cots.append(jnp.concatenate([-(rest_r * fr + rest_i * fi), rest_r * fi - rest_i * fr], 1))
    t = right_mul(jnp.concatenate(cots, 0), a1, a2)
    steps = []
    for a in range(0, STEP, 2):
        cols = []
        for k in (a, a + 1):
            tk = t[k * ROWS : (k + 1) * ROWS]
            cols.append(jnp.concatenate([tk[:, :SIZE], tk[:, SIZE:]], 0))
        dp = left_mul(b1, b2, jnp.concatenate(cols, 1))
        fields = []
        for k in (a, a + 1):
            gr, gi = g_ref[k, 0], g_ref[k, 1]
            power = gr * gr + gi * gi
            scale = 1.0 / jnp.sum(power, keepdims=True)
            dk = dp[:, (k - a) * SIZE : (k - a + 1) * SIZE]
            mean = jnp.sum(dk * power, keepdims=True) * scale
            dk = (dk - mean) * (scale * (4.0 / (SIZE * SIZE)))
            fields.append(jnp.concatenate([gr * dk, gi * dk], 0))
        h = left_mul(e1, e2, jnp.concatenate(fields, 1))
        for k in (a, a + 1):
            lanes = slice((k - a) * SIZE, (k - a + 1) * SIZE)
            steps.append(jnp.concatenate([h[:PUP, lanes], h[PUP:, lanes]], 1))
    dq = right_mul(jnp.concatenate(steps, 0), f1, f2)
    low = low_lanes(PUP // 2)
    flat = []
    for k in range(STEP):
        m = q_ref[k] * pltpu.roll(dq[k * PUP : (k + 1) * PUP], PUP, 1)
        m = m - pltpu.roll(m, PUP, 1)
        dphase = jnp.where(low, m[: PUP // 2], -m[PUP // 2 :])
        if wide:
            out[k] = dphase
        else:
            flat.append(dphase + other[k])
    for at in range(0, FRAMES if flat else 0, STEP):

        @pl.when(step * STEP == at)
        def _(at=at):
            for k, dphase in enumerate(flat):
                for r in range(PUP // 2):
                    out[at + k : at + k + 1, r * SIZE : (r + 1) * SIZE] = dphase[r : r + 1]


def backward(wide, place, q, s, d, g, parts, near, other, tables):
    block = 2 * GROUP
    pairs = pl.BlockSpec((STEP, PUP // 2, SIZE), lambda i: (i, 0, 0))
    if wide:
        sources, specs = list(parts), [whole(p) for p in parts]
        dphase, dphase_spec = shape(FRAMES, PUP // 2, SIZE), pairs
    else:
        sources = list(parts) * 2 + [other]
        specs = [pl.BlockSpec((STEP * block, SIZE), lambda i: (i, 0))] * NY
        specs += [pl.BlockSpec((block, SIZE), lambda i: (FRAMES, 0))] * NY + [pairs]
        dphase = shape(FRAMES, PUP * PUP)
        dphase_spec = pl.BlockSpec(dphase.shape, lambda i: (0, 0))
    return pl.pallas_call(
        functools.partial(backward_kernel, wide),
        grid=(FRAMES // STEP,),
        in_specs=[
            smem(),
            pl.BlockSpec((STEP, PUP, 2 * PUP), lambda i: (i, 0, 0)),
            pl.BlockSpec((STEP, ROWS, 2 * SIZE), lambda i: (i, 0, 0)),
            pl.BlockSpec((STEP, ROWS, 2 * SIZE), lambda i: (i, 0, 0)),
            pl.BlockSpec((STEP, 2, SIZE, SIZE), lambda i: (i, 0, 0, 0)),
        ]
        + specs
        + [whole(near)]
        + [whole(t) for t in tables],
        out_specs=[dphase_spec, pl.BlockSpec((2, SIZE, SIZE), lambda i: (0, 0, 0))],
        out_shape=[dphase, shape(2, SIZE, SIZE)],
        scratch_shapes=[pltpu.VMEM((2, ROWS, SIZE), F32)],
        compiler_params=pltpu.CompilerParams(vmem_limit_bytes=VMEM_LIMIT),
        cost_estimate=pl.CostEstimate(flops=4_000_000_000, bytes_accessed=8_000_000, transcendentals=0),
        name="backward_wide" if wide else "backward_narrow",
    )(place, q, s, d, g, *sources, near, *tables)


def along(axis, shift):
    pairs = []
    for y in range(NY):
        for z in range(NZ):
            to = ((y + shift) % NY, z) if axis == "y" else (y, (z + shift) % NZ)
            pairs.append((y * NZ + z, to[0] * NZ + to[1]))
    return pairs


def send(x, axis, shift):
    return lax.ppermute(x, "chan", along(axis, shift))


def shards(alpha, images, modes, diversity, chan_of_frame):
    tables_f, tables_b = ([jnp.asarray(t) for t in group] for group in make_tables())
    here = lax.axis_index("chan")
    place = jnp.stack([here // NZ, here % NZ]).astype(jnp.int32)
    own_ids = jnp.zeros((8, SIZE), F32).at[0, :FRAMES].set(chan_of_frame[:, 0].astype(F32))

    phase = jnp.dot(alpha, modes, precision=lax.Precision.HIGH).reshape(FRAMES, PUP // 2, SIZE)
    axis = np.arange(PUP, dtype=np.float32) - (PUP - 1) / 2.0
    pupil = (axis[:, None] ** 2 + axis[None, :] ** 2 <= (PUP / 2.0) ** 2).astype(np.float32)
    pupil = jnp.asarray(pupil.reshape(PUP // 2, SIZE))
    extra = [diversity.reshape(PUP // 2, SIZE), own_ids]

    *narrow_kept, n0, n1, n2, n3 = forward(False, place, phase, pupil, extra, images, tables_f)
    *wide_kept, w0, n1, w2, n3 = forward(True, place, phase, pupil, [n1, n3], images, tables_f)
    n2 = send(n2, "y", 2)
    reading = [pltpu.SMEM((2, 8, SIZE), F32), pltpu.SemaphoreType.DMA((2,))]
    first, first_edge = plain(
        first_sum_kernel,
        "sum_first",
        [],
        [n0, n2],
        [shape(32, 3 * GROUP, SIZE), shape(32, 8, SIZE)],
        reading,
        pl.CostEstimate(flops=4_000_000_000, bytes_accessed=2_000_000, transcendentals=0),
    )
    n1, n3 = send(n1, "y", 1), send(n3, "y", 3)
    keep, up, down = plain(
        sum_kernel,
        "sum_channels",
        [place],
        [first, first_edge, n1, n3, w0, send(w2, "y", 2)],
        [shape(rows, SIZE) for rows in (3 * Z_ROWS, UP_ROWS, DOWN_ROWS)],
        [
            pltpu.VMEM((32, 3 * GROUP, SIZE), F32),
            pltpu.VMEM((32, 8, SIZE), F32),
            pltpu.VMEM((Z_ROWS, SIZE), F32),
            pltpu.VMEM((W_ROWS, SIZE), F32),
            *reading,
        ],
    )
    ids = jnp.concatenate([n[base + IDS, :FRAMES] for n, base in zip((n0, n1, n2, n3), BASE, strict=True)])
    ids = ids.astype(jnp.int32)
    up, down = send(up, "z", 1), send(down, "z", -1)
    far, back = plain(relay_kernel, "relay", [], [keep, up, down], [shape(Z_ROWS, SIZE)] * 2, [])
    far, back = send(far, "z", 3), send(back, "z", -3)
    (own,) = plain(object_kernel, "objects", [], [keep, up, down, far, back], [shape(F_ROWS, SIZE)], [])
    ahead, behind = send(own, "z", -3), send(own, "z", 3)
    up = send(jnp.concatenate([own, ahead, behind[:F_FIRST]]), "z", 1)
    down = send(jnp.concatenate([own, behind, ahead[F_FIRST:]]), "z", -1)
    *back, wide_own, near = plain(
        select_kernel,
        "select_objects",
        [place, ids],
        [own, ahead, behind, up, down],
        [shape(R_ROWS, SIZE)] * NY + [shape(2 * GROUP, SIZE), shape(2 * FRAMES + 8, SIZE)],
        [pltpu.VMEM((32, 2 * GROUP, SIZE), F32), pltpu.VMEM((32, 8, SIZE), F32), pltpu.VMEM((2 * GROUP, SIZE), F32), pltpu.VMEM((F_ROWS, SIZE), F32)],
    )
    wide_back = [wide_own] + [send(wide_own, "y", k) for k in range(1, NY)]
    back = [back[0]] + [send(back[k], "y", k) for k in range(1, NY)]

    wide_dphase, wide_object = backward(True, place, *wide_kept, wide_back, near, None, tables_b)
    dphase, narrow_object = backward(False, place, *narrow_kept, back, near, wide_dphase, tables_b)
    gradient = lax.dot_general(dphase, modes, (((1,), (1,)), ((), ())), precision=lax.Precision.HIGH)
    return gradient, narrow_object[None], wide_object


def solution(mesh):
    placed = (
        P(("patch", "chan"), None),
        P(("patch", "chan"), None, None, None),
        P(),
        P(),
        P("chan", None),
    )
    return jax.shard_map(
        shards,
        mesh=mesh,
        in_specs=placed,
        out_specs=(
            P(("patch", "chan"), None),
            P(("patch", "chan"), None, None, None),
            P("patch", None, None),
        ),
        check_vma=False,
    )
```

```python
import functools
import math

import jax
import jax.numpy as jnp
import numpy as np
from jax import lax
from jax.experimental import pallas as pl
from jax.experimental.pallas import tpu as pltpu
from jax.sharding import PartitionSpec as P

PUP = 64
SIZE = 128
HALF = SIZE // 2 + 1
ROWS = 72
NY, NZ = 4, 8
GROUP = 64 // NY
OWN = 32 // NZ
FRAMES = 16
STEP = 16
PRIOR_WEIGHT = 0.1
F32 = jnp.float32
BF16 = jnp.bfloat16
VMEM_LIMIT = 8 * 1024 * 1024
VMEM_SMALL = 4 * 1024 * 1024
EDGES = FRAMES * 3 * GROUP
IDS = EDGES + FRAMES * 3
Y_ROWS = IDS + 8
W_ROWS = 56
BASE = (0, W_ROWS, 0, W_ROWS)
Z_ROWS = 216
F_ROWS = 144
R_ROWS = FRAMES * 2 * GROUP


def dft(length, columns):
    angle = np.outer(np.arange(length), np.arange(columns)) % SIZE * (2.0 * math.pi / SIZE)
    return np.cos(angle), -np.sin(angle)


def halves(table):
    table = np.asarray(table, np.float32)
    high = table.astype(jnp.bfloat16)
    low = (table - high.astype(np.float32)).astype(jnp.bfloat16)
    return high, low


def left_short(table):
    high, low = halves(table)
    return [np.concatenate([high, high], 1), low]


def right_short(table):
    high, low = halves(table)
    return [np.concatenate([high, high], 0), low]


def mirrors():
    rows, lanes = np.zeros((SIZE, SIZE)), np.zeros((SIZE, SIZE))
    for j in range(1, 64):
        rows[j, 64 - j] = 1.0
        rows[64 + j, 128 - j] = -1.0
    for v in range(SIZE):
        lanes[-v % SIZE, v] = 1.0
    return [rows.astype(jnp.bfloat16), lanes.astype(jnp.bfloat16)]


def make_tables():
    c, s = dft(SIZE, SIZE)
    cp, sp = dft(SIZE, PUP)
    order = np.r_[0:PUP:2, 1:PUP:2]
    cx, sx = cp[:, order], sp[:, order]
    ch, sh = np.zeros((ROWS, SIZE)), np.zeros((ROWS, SIZE))
    ch[:HALF], sh[:HALF] = c[:HALF], s[:HALF]
    weight = np.zeros((ROWS, 1))
    weight[:HALF] = 2.0
    weight[0] = weight[HALF - 1] = 1.0
    forward = (
        right_short(np.block([[cp.T, sp.T], [-sp.T, cp.T]]))
        + left_short(np.block([[cx, -sx], [sx, cx]]))
        + left_short(np.concatenate([ch, sh], 0))
        + list(halves(np.block([[c.T, s.T], [-s.T, c.T]])))
    )
    backward = (
        list(halves(np.block([[c, -s], [s, c]])))
        + list(halves(np.concatenate([(weight * ch).T, (weight * sh).T], 1)))
        + list(halves(np.block([[cx.T, sx.T], [-sx.T, cx.T]])))
        + list(halves(np.block([[cp, -sp], [sp, cp]])))
        + mirrors()
    )
    return forward, backward


def mm(a, b):
    return jnp.dot(a, b, preferred_element_type=F32)


def cut(x):
    high = x.astype(BF16)
    return high, (x - high.astype(F32)).astype(BF16)


def right_mul_short(x, twice, low):
    h, r = cut(x)
    return mm(jnp.concatenate([h, r], 1), twice[...]) + mm(h, low[...])


def left_mul_short(twice, low, x):
    h, r = cut(x)
    return mm(twice[...], jnp.concatenate([h, r], 0)) + mm(low[...], h)


def right_mul(x, high, low):
    h, r = cut(x)
    return mm(h, high[...]) + (mm(r, high[...]) + mm(h, low[...]))


def left_mul(high, low, x):
    h, r = cut(x)
    return mm(high[...], h) + (mm(high[...], r) + mm(low[...], h))


def pair_spectra(blocks, left, right):
    out = []
    for a, b in zip(blocks[::2], blocks[1::2], strict=True):
        t = left_mul_short(*left, jnp.concatenate([a, b], 1))
        for k in range(2):
            lanes = slice(k * SIZE, (k + 1) * SIZE)
            out.append(jnp.concatenate([t[:ROWS, lanes], t[ROWS:, lanes]], 1))
    full = right_mul(jnp.concatenate(out, 0), *right)
    return [full[k * ROWS : (k + 1) * ROWS] for k in range(len(blocks))]


def cos_sin(x):
    turns = jnp.floor(x * (2.0 / math.pi) + 0.5)
    r = ((x - turns * 1.5703125) - turns * 4.837512969970703125e-4) - turns * 7.54978995489188216e-8
    z = r * r
    sine = r + r * z * ((-1.9515295891e-4 * z + 8.3321608736e-3) * z - 1.6666654611e-1)
    cosine = 1.0 - 0.5 * z + z * z * ((2.443315711809948e-5 * z - 1.388731625493765e-3) * z + 4.166664568298827e-2)
    quarter = turns.astype(jnp.int32)
    odd = (quarter & 1) != 0
    c, s = jnp.where(odd, sine, cosine), jnp.where(odd, cosine, sine)
    return jnp.where(((quarter + 1) & 2) != 0, -c, c), jnp.where((quarter & 2) != 0, -s, s)


def low_lanes(rows):
    return lax.broadcasted_iota(jnp.int32, (rows, SIZE), 1) < PUP


def forward_kernel(wide, place, phase_ref, pupil_ref, *rest):
    if not wide:
        diversity_ref, ids_ref, *rest = rest
    else:
        _, _, *rest = rest
    im_ref, r1, r2, l1, l2, h1, h2, f1, f2, q_ref, s_ref, d_ref, g_ref, *outs, scr = rest
    step = pl.program_id(0)
    y = place[0]
    low = low_lanes(PUP // 2)
    for k in range(STEP):
        total = phase_ref[k]
        if not wide:
            total = total + diversity_ref[...]
        re, im = (pupil_ref[...] * part for part in cos_sin(total))
        q_ref[k, : PUP // 2, :] = jnp.where(low, re, pltpu.roll(im, PUP, 1))
        q_ref[k, PUP // 2 :, :] = jnp.where(low, pltpu.roll(re, PUP, 1), im)
    t = right_mul_short(q_ref[...].reshape(STEP * PUP, 2 * PUP), r1, r2)
    powers = []
    for a in range(0, STEP, 2):
        cols = []
        for k in (a, a + 1):
            tk = t[k * PUP : (k + 1) * PUP]
            cols.append(jnp.concatenate([tk[:, :SIZE], tk[:, SIZE:]], 0))
        g = left_mul_short(l1, l2, jnp.concatenate(cols, 1))
        for k in (a, a + 1):
            lanes = slice((k - a) * SIZE, (k - a + 1) * SIZE)
            gr, gi = g[:SIZE, lanes], g[SIZE:, lanes]
            g_ref[k, 0], g_ref[k, 1] = gr, gi
            power = gr * gr + gi * gi
            powers.append(power * (1.0 / jnp.sum(power, keepdims=True)))
    images = [im_ref[k, 0] for k in range(STEP)]
    spectra = pair_spectra(powers + images, (h1, h2), (f1, f2))

    if wide:

        @pl.when(step == 0)
        def _():
            scr[...] = jnp.zeros_like(scr)

    for k in range(STEP):
        sk, dk = spectra[k], spectra[STEP + k] * (1.0 / SIZE)
        s_ref[k], d_ref[k] = sk, dk
        sr, si, dr, di = sk[:, :SIZE], sk[:, SIZE:], dk[:, :SIZE], dk[:, SIZE:]
        terms = (dr * sr + di * si, di * sr - dr * si, sr * sr + si * si)
        for c in range(3):
            if wide:
                scr[c] += terms[c]
            else:
                scr[c] = terms[c]
        if not wide:
            frame = step * STEP + k
            for shift in range(NY):
                row = pl.multiple_of(GROUP * lax.rem(y + shift, NY), GROUP)
                for c in range(3):
                    at = pl.multiple_of(BASE[shift] + frame * 3 * GROUP + c * GROUP, 8)
                    outs[shift][pl.ds(at, GROUP), :] = scr[c, pl.ds(row, GROUP), :]
                    outs[shift][pl.ds(BASE[shift] + EDGES + 3 * frame + c, 1), :] = scr[c, 64:65, :]

    @pl.when(step == 0)
    def _():
        if not wide:
            for shift in range(NY):
                outs[shift][BASE[shift] + IDS :, :] = ids_ref[...]

    if wide:

        @pl.when(step == FRAMES // STEP - 1)
        def _():
            for shift in range(NY):
                out = outs[shift]
                row = pl.multiple_of(GROUP * lax.rem(y + shift, NY), GROUP)
                for c in range(3):
                    out[c * GROUP : (c + 1) * GROUP, :] = scr[c, pl.ds(row, GROUP), :]
                    out[3 * GROUP + c : 3 * GROUP + c + 1, :] = scr[c, 64:65, :]
                out[3 * GROUP + 3 :, :] = jnp.zeros((W_ROWS - 3 * GROUP - 3, SIZE), F32)


def smem():
    return pl.BlockSpec(memory_space=pltpu.SMEM)


def whole(a):
    return pl.BlockSpec(a.shape, lambda i: (0,) * a.ndim)


def shape(*dims):
    return jax.ShapeDtypeStruct(dims, F32)


def forward(wide, place, phase, pupil, extra, images, tables):
    camera = 0 if wide else 1
    outs = [shape(FRAMES, PUP, 2 * PUP)] + [shape(FRAMES, ROWS, 2 * SIZE)] * 2 + [shape(FRAMES, 2, SIZE, SIZE)]
    terms = [shape(W_ROWS if wide and not base else Y_ROWS + base, SIZE) for base in BASE]
    return pl.pallas_call(
        functools.partial(forward_kernel, wide),
        grid=(FRAMES // STEP,),
        in_specs=[smem(), pl.BlockSpec((STEP, PUP // 2, SIZE), lambda i: (i, 0, 0)), whole(pupil)]
        + [pl.BlockSpec(memory_space=pl.ANY) if wide else whole(e) for e in extra]
        + [pl.BlockSpec((STEP, 1, SIZE, SIZE), lambda i: (i, camera, 0, 0))]
        + [whole(t) for t in tables],
        out_specs=[pl.BlockSpec((STEP, PUP, 2 * PUP), lambda i: (i, 0, 0))]
        + [pl.BlockSpec((STEP, ROWS, 2 * SIZE), lambda i: (i, 0, 0))] * 2
        + [pl.BlockSpec((STEP, 2, SIZE, SIZE), lambda i: (i, 0, 0, 0))]
        + [pl.BlockSpec((W_ROWS, SIZE), lambda i: (0, 0)) if wide else whole(t) for t in terms],
        out_shape=outs + terms,
        input_output_aliases={3: len(outs) + 1, 4: len(outs) + 3} if wide else {},
        scratch_shapes=[pltpu.VMEM((3, ROWS, SIZE), F32)],
        compiler_params=pltpu.CompilerParams(vmem_limit_bytes=VMEM_LIMIT),
        cost_estimate=pl.CostEstimate(flops=4_000_000_000, bytes_accessed=8_000_000, transcendentals=0),
        name="forward_wide" if wide else "forward_narrow",
    )(place, phase, pupil, *extra, images, *tables)


UP, DOWN, KEEP = (1, 6, 4), (7, 2, 4), (0, 3, 5)
Z_FIRST, F_FIRST = 112, 72
UP_ROWS, DOWN_ROWS = 2 * Z_ROWS + Z_FIRST, 3 * Z_ROWS - Z_FIRST


def number_copies(sources, bases, numbers, arrived):
    return [
        pltpu.make_async_copy(source.at[pl.ds(base + IDS, 8)], numbers.at[n], arrived.at[n])
        for n, (source, base) in enumerate(zip(sources, bases, strict=True))
    ]


def add_frames(sources, bases, acc, edge, numbers):
    for n, (source, base) in enumerate(zip(sources, bases, strict=True)):
        for f in range(FRAMES):
            k = numbers[n, 0, f].astype(jnp.int32)
            at = base + f * 3 * GROUP
            acc[k] += source[at : at + 3 * GROUP, :]
            at = base + EDGES + 3 * f
            edge[k, 0:3, :] += source[at : at + 3, :]


def first_sum_kernel(n0, n2, acc, edge, numbers, arrived):
    copies = number_copies((n0, n2), (BASE[0], BASE[2]), numbers, arrived)
    for copy in copies:
        copy.start()
    acc[...] = jnp.zeros_like(acc)
    edge[...] = jnp.zeros_like(edge)
    for copy in copies:
        copy.wait()
    add_frames((n0, n2), (BASE[0], BASE[2]), acc, edge, numbers)


def sum_kernel(place, first, first_edge, n1, n3, w0, w2, keep, up, down, acc, edge, block, total, numbers, arrived):
    z = place[1]
    copies = number_copies((n1, n3), (BASE[1], BASE[3]), numbers, arrived)
    for copy in copies:
        copy.start()
    acc[...] = first[...]
    edge[...] = first_edge[...]
    total[...] = (w0[...] + w2[...]) + (n1[:W_ROWS, :] + n3[:W_ROWS, :])
    for copy in copies:
        copy.wait()
    add_frames((n1, n3), (BASE[1], BASE[3]), acc, edge, numbers)

    def pack(out, group):
        for n, shift in enumerate(group):
            to = lax.rem(z + shift, NZ)
            start = n * Z_ROWS
            for k in range(OWN):
                at = start + k * 3 * GROUP
                out[at : at + 3 * GROUP, :] = acc[OWN * to + k]
                at = start + OWN * 3 * GROUP + 3 * k
                out[at : at + 3, :] = edge[OWN * to + k, 0:3, :]
            at = start + OWN * (3 * GROUP + 3)
            for c in range(3):
                for j in range(2):
                    row = pl.ds(GROUP * c + 2 * to + j, 1)
                    out[at + 2 * c + j : at + 2 * c + j + 1, :] = total[row, :]
            row = slice(3 * GROUP, 3 * GROUP + 3)
            out[at + 6 : at + 9, :] = total[row, :]
            out[at + 9 : start + Z_ROWS, :] = jnp.zeros((Z_ROWS - OWN * (3 * GROUP + 3) - 9, SIZE), F32)

    pack(keep, KEEP)
    pack(up, UP[:2])
    pack(down, DOWN[:2])
    pack(block, UP[2:])
    up[2 * Z_ROWS :, :] = block[:Z_FIRST, :]
    down[2 * Z_ROWS :, :] = block[Z_FIRST:, :]


def relay_kernel(keep, up, down, far, back):
    end = 2 * Z_ROWS
    far[:Z_FIRST, :] = keep[Z_ROWS : Z_ROWS + Z_FIRST, :] + (up[end:, :] + down[Z_ROWS : Z_ROWS + Z_FIRST, :])
    far[Z_FIRST:, :] = keep[Z_ROWS + Z_FIRST : end, :] + down[Z_ROWS + Z_FIRST : end, :]
    back[:Z_FIRST, :] = keep[end : end + Z_FIRST, :] + up[Z_ROWS : Z_ROWS + Z_FIRST, :]
    back[Z_FIRST:, :] = keep[end + Z_FIRST :, :] + (up[Z_ROWS + Z_FIRST : end, :] + down[end:, :])


def quotient(num_re, num_im, den):
    den = PRIOR_WEIGHT + den
    return num_re / den, num_im / den


def object_kernel(keep, up, down, far, back, out):
    own = slice(0, Z_ROWS)
    sums = (keep[own, :] + (up[own, :] + down[own, :])) + (far[...] + back[...])
    for k in range(OWN):
        base = k * 3 * GROUP
        re, im = quotient(*(sums[base + c * GROUP : base + (c + 1) * GROUP] for c in range(3)))
        out[k * 2 * GROUP : k * 2 * GROUP + GROUP, :] = re
        out[k * 2 * GROUP + GROUP : (k + 1) * 2 * GROUP, :] = im
        base = OWN * 3 * GROUP + 3 * k
        re, im = quotient(*(sums[base + c : base + c + 1] for c in range(3)))
        at = OWN * 2 * GROUP + 2 * k
        out[at : at + 1, :] = re
        out[at + 1 : at + 2, :] = im
    base = OWN * (3 * GROUP + 3)
    at = OWN * (2 * GROUP + 2)
    re, im = quotient(*(sums[base + 2 * c : base + 2 * c + 2] for c in range(3)))
    out[at : at + 2, :] = re
    out[at + 2 : at + 4, :] = im
    re, im = quotient(*(sums[base + 6 + c : base + 7 + c] for c in range(3)))
    out[at + 4 : at + 5, :] = re
    out[at + 5 : at + 6, :] = im
    out[at + 6 :, :] = jnp.zeros((F_ROWS - at - 6, SIZE), F32)


def select_kernel(place, ids, own, ahead, behind, up, down, *refs):
    outs, wides, (near, objects, edge, total, other) = refs[:NY], refs[NY : 2 * NY], refs[2 * NY :]
    other[:F_FIRST, :] = up[2 * F_ROWS :, :]
    other[F_FIRST:, :] = down[2 * F_ROWS :, :]
    y, z = place[0], place[1]
    parts = ((0, own, 0), (3, ahead, 0), (5, behind, 0), (7, up, 0), (2, up, 1), (1, down, 0), (6, down, 1), (4, other, 0))
    for shift, part, n in parts:
        source = lax.rem(z + shift, NZ)
        start = n * F_ROWS
        for k in range(OWN):
            at = start + k * 2 * GROUP
            objects[OWN * source + k] = part[at : at + 2 * GROUP, :]
            at = start + OWN * 2 * GROUP + 2 * k
            edge[OWN * source + k, 0:2, :] = part[at : at + 2, :]
        at = start + OWN * (2 * GROUP + 2)
        for j in range(2):
            total[pl.ds(2 * source + j, 1), :] = part[at + j : at + j + 1, :]
            total[pl.ds(GROUP + 2 * source + j, 1), :] = part[at + 2 + j : at + 3 + j, :]
    for shift in range(NY):
        out = outs[shift]
        start = (NY - shift) % NY * FRAMES
        for f in range(FRAMES):
            out[f * 2 * GROUP : (f + 1) * 2 * GROUP, :] = objects[ids[start + f]]
        wides[shift][: 2 * GROUP, :] = objects[lax.rem(y + shift, NY) * NZ + z]
        wides[shift][2 * GROUP :, :] = total[...]
    for f in range(FRAMES):
        near[2 * f : 2 * f + 2, :] = edge[ids[f], 0:2, :]
    near[2 * FRAMES : 2 * FRAMES + 2, :] = edge[y * NZ + z, 0:2, :]
    at = OWN * (2 * GROUP + 2) + 4
    near[2 * FRAMES + 2 : 2 * FRAMES + 4, :] = own[at : at + 2, :]
    near[2 * FRAMES + 4 :, :] = jnp.zeros((4, SIZE), F32)


def plain(kernel, name, smems, arrays, outs, scratch, cost=None):
    return pl.pallas_call(
        kernel,
        in_specs=[smem()] * len(smems) + [pl.BlockSpec(memory_space=pltpu.VMEM)] * len(arrays),
        out_specs=[pl.BlockSpec(memory_space=pltpu.VMEM)] * len(outs),
        out_shape=outs,
        scratch_shapes=scratch,
        compiler_params=pltpu.CompilerParams(vmem_limit_bytes=VMEM_SMALL),
        cost_estimate=cost,
        name=name,
    )(*smems, *arrays)


def backward_kernel(wide, place, q_ref, s_ref, d_ref, g_ref, *refs):
    parts, refs = refs[:NY], refs[NY:]
    if not wide:
        other, *refs = refs
    near, a1, a2, b1, b2, e1, e2, f1, f2, m1, m2, out, *objs, scr = refs
    step = pl.program_id(0)
    y = place[0]

    def gather(sources, at):
        for shift in range(NY):
            row = pl.multiple_of(GROUP * lax.rem(y + NY - shift, NY), GROUP)
            for c in range(2):
                scr[c, pl.ds(row, GROUP), :] = sources[shift][at + c * GROUP : at + (c + 1) * GROUP, :]

    @pl.when(step == 0)
    def _():
        scr[...] = jnp.zeros_like(scr)
        for item, obj in enumerate(objs):
            gather(parts, item * 2 * GROUP)
            at = 2 * (FRAMES + item)
            for c in range(2):
                scr[c, 64:65, :] = near[at + c : at + c + 1, :]
            half = jnp.concatenate([scr[0, :64, :], scr[1, :64, :]], 0)
            high = half.astype(BF16)
            middle, low = cut(half - high.astype(F32))
            turned = jnp.zeros((SIZE, SIZE), F32)
            for part in (high, middle, low):
                turned = turned + mm(m1[...], mm(part, m2[...]).astype(BF16))
            for c in range(2):
                obj[c, :64, :] = scr[c, :64, :]
                obj[c, 64:, :] = turned[64 * c : 64 * (c + 1)]
                obj[c, 64:65, :] = scr[c, 64:65, :]

    cots = []
    for k in range(STEP):
        if not wide:
            gather(parts, k * 2 * GROUP)
            for c in range(2):
                scr[c, 64:65, :] = near[pl.ds(2 * (step * STEP + k) + c, 1), :]
        fr, fi = scr[0], scr[1]
        sk, dk = s_ref[k], d_ref[k]
        sr, si, dr, di = sk[:, :SIZE], sk[:, SIZE:], dk[:, :SIZE], dk[:, SIZE:]
        rest_r = dr - (fr * sr - fi * si)
        rest_i = di - (fr * si + fi * sr)
        cots.append(jnp.concatenate([-(rest_r * fr + rest_i * fi), rest_r * fi - rest_i * fr], 1))
    t = right_mul(jnp.concatenate(cots, 0), a1, a2)
    steps = []
    for a in range(0, STEP, 2):
        cols = []
        for k in (a, a + 1):
            tk = t[k * ROWS : (k + 1) * ROWS]
            cols.append(jnp.concatenate([tk[:, :SIZE], tk[:, SIZE:]], 0))
        dp = left_mul(b1, b2, jnp.concatenate(cols, 1))
        fields = []
        for k in (a, a + 1):
            gr, gi = g_ref[k, 0], g_ref[k, 1]
            power = gr * gr + gi * gi
            scale = 1.0 / jnp.sum(power, keepdims=True)
            dk = dp[:, (k - a) * SIZE : (k - a + 1) * SIZE]
            mean = jnp.sum(dk * power, keepdims=True) * scale
            dk = (dk - mean) * (scale * (4.0 / (SIZE * SIZE)))
            fields.append(jnp.concatenate([gr * dk, gi * dk], 0))
        h = left_mul(e1, e2, jnp.concatenate(fields, 1))
        for k in (a, a + 1):
            lanes = slice((k - a) * SIZE, (k - a + 1) * SIZE)
            steps.append(jnp.concatenate([h[:PUP, lanes], h[PUP:, lanes]], 1))
    dq = right_mul(jnp.concatenate(steps, 0), f1, f2)
    low = low_lanes(PUP // 2)
    flat = []
    for k in range(STEP):
        m = q_ref[k] * pltpu.roll(dq[k * PUP : (k + 1) * PUP], PUP, 1)
        m = m - pltpu.roll(m, PUP, 1)
        dphase = jnp.where(low, m[: PUP // 2], -m[PUP // 2 :])
        if wide:
            out[k] = dphase
        else:
            flat.append(dphase + other[k])
    for at in range(0, FRAMES if flat else 0, STEP):

        @pl.when(step * STEP == at)
        def _(at=at):
            for k, dphase in enumerate(flat):
                for r in range(PUP // 2):
                    out[at + k : at + k + 1, r * SIZE : (r + 1) * SIZE] = dphase[r : r + 1]


def backward(wide, place, q, s, d, g, parts, near, other, tables):
    block = 2 * GROUP
    pairs = pl.BlockSpec((STEP, PUP // 2, SIZE), lambda i: (i, 0, 0))
    if wide:
        sources, specs = list(parts), [whole(p) for p in parts]
        dphase, dphase_spec = shape(FRAMES, PUP // 2, SIZE), pairs
    else:
        sources = list(parts) + [other]
        specs = [pl.BlockSpec((STEP * block, SIZE), lambda i: (i, 0))] * NY
        specs += [pairs]
        dphase = shape(FRAMES, PUP * PUP)
        dphase_spec = pl.BlockSpec(dphase.shape, lambda i: (0, 0))
    return pl.pallas_call(
        functools.partial(backward_kernel, wide),
        grid=(FRAMES // STEP,),
        in_specs=[
            smem(),
            pl.BlockSpec((STEP, PUP, 2 * PUP), lambda i: (i, 0, 0)),
            pl.BlockSpec((STEP, ROWS, 2 * SIZE), lambda i: (i, 0, 0)),
            pl.BlockSpec((STEP, ROWS, 2 * SIZE), lambda i: (i, 0, 0)),
            pl.BlockSpec((STEP, 2, SIZE, SIZE), lambda i: (i, 0, 0, 0)),
        ]
        + specs
        + [whole(near)]
        + [whole(t) for t in tables],
        out_specs=[dphase_spec] + [pl.BlockSpec((2, SIZE, SIZE), lambda i: (0, 0, 0))] * (2 * wide),
        out_shape=[dphase] + [shape(2, SIZE, SIZE)] * (2 * wide),
        scratch_shapes=[pltpu.VMEM((2, ROWS, SIZE), F32)],
        compiler_params=pltpu.CompilerParams(vmem_limit_bytes=VMEM_LIMIT),
        cost_estimate=pl.CostEstimate(flops=4_000_000_000, bytes_accessed=8_000_000, transcendentals=0),
        name="backward_wide" if wide else "backward_narrow",
    )(place, q, s, d, g, *sources, near, *tables)


def along(axis, shift):
    pairs = []
    for y in range(NY):
        for z in range(NZ):
            to = ((y + shift) % NY, z) if axis == "y" else (y, (z + shift) % NZ)
            pairs.append((y * NZ + z, to[0] * NZ + to[1]))
    return pairs


def send(x, axis, shift):
    return lax.ppermute(x, "chan", along(axis, shift))


def shards(alpha, images, modes, diversity, chan_of_frame):
    tables_f, tables_b = ([jnp.asarray(t) for t in group] for group in make_tables())
    here = lax.axis_index("chan")
    place = jnp.stack([here // NZ, here % NZ]).astype(jnp.int32)
    own_ids = jnp.zeros((8, SIZE), F32).at[0, :FRAMES].set(chan_of_frame[:, 0].astype(F32))

    phase = jnp.dot(alpha, modes, precision=lax.Precision.HIGH).reshape(FRAMES, PUP // 2, SIZE)
    axis = np.arange(PUP, dtype=np.float32) - (PUP - 1) / 2.0
    pupil = (axis[:, None] ** 2 + axis[None, :] ** 2 <= (PUP / 2.0) ** 2).astype(np.float32)
    pupil = jnp.asarray(pupil.reshape(PUP // 2, SIZE))
    extra = [diversity.reshape(PUP // 2, SIZE), own_ids]

    *narrow_kept, n0, n1, n2, n3 = forward(False, place, phase, pupil, extra, images, tables_f)
    *wide_kept, w0, n1, w2, n3 = forward(True, place, phase, pupil, [n1, n3], images, tables_f)
    n2 = send(n2, "y", 2)
    reading = [pltpu.SMEM((2, 8, SIZE), F32), pltpu.SemaphoreType.DMA((2,))]
    first, first_edge = plain(
        first_sum_kernel,
        "sum_first",
        [],
        [n0, n2],
        [shape(32, 3 * GROUP, SIZE), shape(32, 8, SIZE)],
        reading,
        pl.CostEstimate(flops=4_000_000_000, bytes_accessed=2_000_000, transcendentals=0),
    )
    n1, n3 = send(n1, "y", 1), send(n3, "y", 3)
    keep, up, down = plain(
        sum_kernel,
        "sum_channels",
        [place],
        [first, first_edge, n1, n3, w0, send(w2, "y", 2)],
        [shape(rows, SIZE) for rows in (3 * Z_ROWS, UP_ROWS, DOWN_ROWS)],
        [
            pltpu.VMEM((32, 3 * GROUP, SIZE), F32),
            pltpu.VMEM((32, 8, SIZE), F32),
            pltpu.VMEM((Z_ROWS, SIZE), F32),
            pltpu.VMEM((W_ROWS, SIZE), F32),
            *reading,
        ],
    )
    ids = jnp.concatenate([n[base + IDS, :FRAMES] for n, base in zip((n0, n1, n2, n3), BASE, strict=True)])
    ids = ids.astype(jnp.int32)
    up, down = send(up, "z", 1), send(down, "z", -1)
    far, back = plain(relay_kernel, "relay", [], [keep, up, down], [shape(Z_ROWS, SIZE)] * 2, [])
    far, back = send(far, "z", 3), send(back, "z", -3)
    (own,) = plain(object_kernel, "objects", [], [keep, up, down, far, back], [shape(F_ROWS, SIZE)], [])
    ahead, behind = send(own, "z", -3), send(own, "z", 3)
    up = send(jnp.concatenate([own, ahead, behind[:F_FIRST]]), "z", 1)
    down = send(jnp.concatenate([own, behind, ahead[F_FIRST:]]), "z", -1)
    *back, near = plain(
        select_kernel,
        "select_objects",
        [place, ids],
        [own, ahead, behind, up, down],
        [shape(R_ROWS, SIZE)] * NY + [shape(4 * GROUP, SIZE)] * NY + [shape(2 * FRAMES + 8, SIZE)],
        [pltpu.VMEM((32, 2 * GROUP, SIZE), F32), pltpu.VMEM((32, 8, SIZE), F32), pltpu.VMEM((2 * GROUP, SIZE), F32), pltpu.VMEM((F_ROWS, SIZE), F32)],
    )
    back, wide_back = back[:NY], back[NY:]
    wide_back = [wide_back[0]] + [send(wide_back[k], "y", k) for k in range(1, NY)]
    back = [back[0]] + [send(back[k], "y", k) for k in range(1, NY)]

    wide_dphase, narrow_object, wide_object = backward(True, place, *wide_kept, wide_back, near, None, tables_b)
    (dphase,) = backward(False, place, *narrow_kept, back, near, wide_dphase, tables_b)
    gradient = lax.dot_general(dphase, modes, (((1,), (1,)), ((), ())), precision=lax.Precision.HIGH)
    return gradient, narrow_object[None], wide_object


def solution(mesh):
    placed = (
        P(("patch", "chan"), None),
        P(("patch", "chan"), None, None, None),
        P(),
        P(),
        P("chan", None),
    )
    return jax.shard_map(
        shards,
        mesh=mesh,
        in_specs=placed,
        out_specs=(
            P(("patch", "chan"), None),
            P(("patch", "chan"), None, None, None),
            P("patch", None, None),
        ),
        check_vma=False,
    )
```

```python
import functools
import math

import jax
import jax.numpy as jnp
import numpy as np
from jax import lax
from jax.experimental import pallas as pl
from jax.experimental.pallas import tpu as pltpu
from jax.sharding import PartitionSpec as P

PUP = 64
SIZE = 128
HALF = SIZE // 2 + 1
ROWS = 72
NY, NZ = 4, 8
GROUP = 64 // NY
OWN = 32 // NZ
FRAMES = 16
STEP = 16
PRIOR_WEIGHT = 0.1
F32 = jnp.float32
BF16 = jnp.bfloat16
VMEM_LIMIT = 8 * 1024 * 1024
VMEM_SMALL = 4 * 1024 * 1024
EDGES = FRAMES * 3 * GROUP
IDS = EDGES + FRAMES * 3
Y_ROWS = IDS + 8
W_ROWS = 56
BASE = (0, W_ROWS, 0, W_ROWS)
Z_ROWS = 216
F_ROWS = 144
R_ROWS = FRAMES * 2 * GROUP


def dft(length, columns):
    angle = np.outer(np.arange(length), np.arange(columns)) % SIZE * (2.0 * math.pi / SIZE)
    return np.cos(angle), -np.sin(angle)


def halves(table):
    table = np.asarray(table, np.float32)
    high = table.astype(jnp.bfloat16)
    low = (table - high.astype(np.float32)).astype(jnp.bfloat16)
    return high, low


def left_short(table):
    high, low = halves(table)
    return [np.concatenate([high, high], 1), low]


def right_short(table):
    high, low = halves(table)
    return [np.concatenate([high, high], 0), low]


def mirrors():
    rows, lanes = np.zeros((SIZE, SIZE)), np.zeros((SIZE, SIZE))
    for j in range(1, 64):
        rows[j, 64 - j] = 1.0
        rows[64 + j, 128 - j] = -1.0
    for v in range(SIZE):
        lanes[-v % SIZE, v] = 1.0
    return [rows.astype(jnp.bfloat16), lanes.astype(jnp.bfloat16)]


def make_tables():
    c, s = dft(SIZE, SIZE)
    cp, sp = dft(SIZE, PUP)
    order = np.r_[0:PUP:2, 1:PUP:2]
    cx, sx = cp[:, order], sp[:, order]
    ch, sh = np.zeros((ROWS, SIZE)), np.zeros((ROWS, SIZE))
    ch[:HALF], sh[:HALF] = c[:HALF], s[:HALF]
    weight = np.zeros((ROWS, 1))
    weight[:HALF] = 2.0
    weight[0] = weight[HALF - 1] = 1.0
    forward = (
        right_short(np.block([[cp.T, sp.T], [-sp.T, cp.T]]))
        + left_short(np.block([[cx, -sx], [sx, cx]]))
        + left_short(np.concatenate([ch, sh], 0))
        + list(halves(np.block([[c.T, s.T], [-s.T, c.T]])))
    )
    backward = (
        list(halves(np.block([[c, -s], [s, c]])))
        + list(halves(np.concatenate([(weight * ch).T, (weight * sh).T], 1)))
        + list(halves(np.block([[cx.T, sx.T], [-sx.T, cx.T]])))
        + list(halves(np.block([[cp, -sp], [sp, cp]])))
        + mirrors()
    )
    return forward, backward


def mm(a, b):
    return jnp.dot(a, b, preferred_element_type=F32)


def cut(x):
    high = x.astype(BF16)
    return high, (x - high.astype(F32)).astype(BF16)


def right_mul_short(x, twice, low):
    h, r = cut(x)
    return mm(jnp.concatenate([h, r], 1), twice[...]) + mm(h, low[...])


def left_mul_short(twice, low, x):
    h, r = cut(x)
    return mm(twice[...], jnp.concatenate([h, r], 0)) + mm(low[...], h)


def right_mul(x, high, low):
    h, r = cut(x)
    return mm(h, high[...]) + (mm(r, high[...]) + mm(h, low[...]))


def left_mul(high, low, x):
    h, r = cut(x)
    return mm(high[...], h) + (mm(high[...], r) + mm(low[...], h))


def pair_spectra(blocks, left, right):
    out = []
    for a, b in zip(blocks[::2], blocks[1::2], strict=True):
        t = left_mul_short(*left, jnp.concatenate([a, b], 1))
        for k in range(2):
            lanes = slice(k * SIZE, (k + 1) * SIZE)
            out.append(jnp.concatenate([t[:ROWS, lanes], t[ROWS:, lanes]], 1))
    full = right_mul(jnp.concatenate(out, 0), *right)
    return [full[k * ROWS : (k + 1) * ROWS] for k in range(len(blocks))]


def cos_sin(x):
    turns = jnp.floor(x * (2.0 / math.pi) + 0.5)
    r = ((x - turns * 1.5703125) - turns * 4.837512969970703125e-4) - turns * 7.54978995489188216e-8
    z = r * r
    sine = r + r * z * ((-1.9515295891e-4 * z + 8.3321608736e-3) * z - 1.6666654611e-1)
    cosine = 1.0 - 0.5 * z + z * z * ((2.443315711809948e-5 * z - 1.388731625493765e-3) * z + 4.166664568298827e-2)
    quarter = turns.astype(jnp.int32)
    odd = (quarter & 1) != 0
    c, s = jnp.where(odd, sine, cosine), jnp.where(odd, cosine, sine)
    return jnp.where(((quarter + 1) & 2) != 0, -c, c), jnp.where((quarter & 2) != 0, -s, s)


def low_lanes(rows):
    return lax.broadcasted_iota(jnp.int32, (rows, SIZE), 1) < PUP


def forward_kernel(wide, place, phase_ref, pupil_ref, *rest):
    if not wide:
        diversity_ref, ids_ref, *rest = rest
    else:
        _, _, *rest = rest
    im_ref, r1, r2, l1, l2, h1, h2, f1, f2, q_ref, s_ref, d_ref, g_ref, *outs, scr = rest
    step = pl.program_id(0)
    y = place[0]
    low = low_lanes(PUP // 2)
    for k in range(STEP):
        total = phase_ref[k]
        if not wide:
            total = total + diversity_ref[...]
        re, im = (pupil_ref[...] * part for part in cos_sin(total))
        q_ref[k, : PUP // 2, :] = jnp.where(low, re, pltpu.roll(im, PUP, 1))
        q_ref[k, PUP // 2 :, :] = jnp.where(low, pltpu.roll(re, PUP, 1), im)
    t = right_mul_short(q_ref[...].reshape(STEP * PUP, 2 * PUP), r1, r2)
    powers = []
    for a in range(0, STEP, 2):
        cols = []
        for k in (a, a + 1):
            tk = t[k * PUP : (k + 1) * PUP]
            cols.append(jnp.concatenate([tk[:, :SIZE], tk[:, SIZE:]], 0))
        g = left_mul_short(l1, l2, jnp.concatenate(cols, 1))
        for k in (a, a + 1):
            lanes = slice((k - a) * SIZE, (k - a + 1) * SIZE)
            gr, gi = g[:SIZE, lanes], g[SIZE:, lanes]
            g_ref[k, 0], g_ref[k, 1] = gr, gi
            power = gr * gr + gi * gi
            powers.append(power * (1.0 / jnp.sum(power, keepdims=True)))
    images = [im_ref[k, 0] for k in range(STEP)]
    spectra = pair_spectra(powers + images, (h1, h2), (f1, f2))

    if wide:

        @pl.when(step == 0)
        def _():
            scr[...] = jnp.zeros_like(scr)

    for k in range(STEP):
        sk, dk = spectra[k], spectra[STEP + k] * (1.0 / SIZE)
        s_ref[k], d_ref[k] = sk, dk
        sr, si, dr, di = sk[:, :SIZE], sk[:, SIZE:], dk[:, :SIZE], dk[:, SIZE:]
        terms = (dr * sr + di * si, di * sr - dr * si, sr * sr + si * si)
        for c in range(3):
            if wide:
                scr[c] += terms[c]
            else:
                scr[c] = terms[c]
        if not wide:
            frame = step * STEP + k
            for shift in range(NY):
                row = pl.multiple_of(GROUP * lax.rem(y + shift, NY), GROUP)
                for c in range(3):
                    at = pl.multiple_of(BASE[shift] + frame * 3 * GROUP + c * GROUP, 8)
                    outs[shift][pl.ds(at, GROUP), :] = scr[c, pl.ds(row, GROUP), :]
                    outs[shift][pl.ds(BASE[shift] + EDGES + 3 * frame + c, 1), :] = scr[c, 64:65, :]

    @pl.when(step == 0)
    def _():
        if not wide:
            for shift in range(NY):
                outs[shift][BASE[shift] + IDS :, :] = ids_ref[...]

    if wide:

        @pl.when(step == FRAMES // STEP - 1)
        def _():
            for shift in range(NY):
                out = outs[shift]
                row = pl.multiple_of(GROUP * lax.rem(y + shift, NY), GROUP)
                for c in range(3):
                    out[c * GROUP : (c + 1) * GROUP, :] = scr[c, pl.ds(row, GROUP), :]
                    out[3 * GROUP + c : 3 * GROUP + c + 1, :] = scr[c, 64:65, :]
                out[3 * GROUP + 3 :, :] = jnp.zeros((W_ROWS - 3 * GROUP - 3, SIZE), F32)


def smem():
    return pl.BlockSpec(memory_space=pltpu.SMEM)


def whole(a):
    return pl.BlockSpec(a.shape, lambda i: (0,) * a.ndim)


def shape(*dims):
    return jax.ShapeDtypeStruct(dims, F32)


def forward(wide, place, phase, pupil, extra, images, tables):
    outs = [shape(FRAMES, PUP, 2 * PUP)] + [shape(FRAMES, ROWS, 2 * SIZE)] * 2 + [shape(FRAMES, 2, SIZE, SIZE)]
    terms = [shape(W_ROWS if wide and not base else Y_ROWS + base, SIZE) for base in BASE]
    return pl.pallas_call(
        functools.partial(forward_kernel, wide),
        grid=(FRAMES // STEP,),
        in_specs=[smem(), pl.BlockSpec((STEP, PUP // 2, SIZE), lambda i: (i, 0, 0)), whole(pupil)]
        + [pl.BlockSpec(memory_space=pl.ANY) if wide else whole(e) for e in extra]
        + [pl.BlockSpec((STEP, 1, SIZE, SIZE), lambda i: (i, 0, 0, 0))]
        + [whole(t) for t in tables],
        out_specs=[pl.BlockSpec((STEP, PUP, 2 * PUP), lambda i: (i, 0, 0))]
        + [pl.BlockSpec((STEP, ROWS, 2 * SIZE), lambda i: (i, 0, 0))] * 2
        + [pl.BlockSpec((STEP, 2, SIZE, SIZE), lambda i: (i, 0, 0, 0))]
        + [pl.BlockSpec((W_ROWS, SIZE), lambda i: (0, 0)) if wide else whole(t) for t in terms],
        out_shape=outs + terms,
        input_output_aliases={3: len(outs) + 1, 4: len(outs) + 3} if wide else {},
        scratch_shapes=[pltpu.VMEM((3, ROWS, SIZE), F32)],
        compiler_params=pltpu.CompilerParams(vmem_limit_bytes=VMEM_LIMIT),
        cost_estimate=pl.CostEstimate(flops=4_000_000_000, bytes_accessed=8_000_000, transcendentals=0),
        name="forward_wide" if wide else "forward_narrow",
    )(place, phase, pupil, *extra, images, *tables)


UP, DOWN, KEEP = (1, 6, 4), (7, 2, 4), (0, 3, 5)
Z_FIRST, F_FIRST = 112, 72
UP_ROWS, DOWN_ROWS = 2 * Z_ROWS + Z_FIRST, 3 * Z_ROWS - Z_FIRST


def number_copies(sources, bases, numbers, arrived):
    return [
        pltpu.make_async_copy(source.at[pl.ds(base + IDS, 8)], numbers.at[n], arrived.at[n])
        for n, (source, base) in enumerate(zip(sources, bases, strict=True))
    ]


def add_frames(sources, bases, acc, edge, numbers):
    for n, (source, base) in enumerate(zip(sources, bases, strict=True)):
        for f in range(FRAMES):
            k = numbers[n, 0, f].astype(jnp.int32)
            at = base + f * 3 * GROUP
            acc[k] += source[at : at + 3 * GROUP, :]
            at = base + EDGES + 3 * f
            edge[k, 0:3, :] += source[at : at + 3, :]


def first_sum_kernel(n0, n2, acc, edge, numbers, arrived):
    copies = number_copies((n0, n2), (BASE[0], BASE[2]), numbers, arrived)
    for copy in copies:
        copy.start()
    acc[...] = jnp.zeros_like(acc)
    edge[...] = jnp.zeros_like(edge)
    for copy in copies:
        copy.wait()
    add_frames((n0, n2), (BASE[0], BASE[2]), acc, edge, numbers)


def sum_kernel(place, first, first_edge, n1, n3, w0, w2, keep, up, down, acc, edge, block, total, numbers, arrived):
    z = place[1]
    copies = number_copies((n1, n3), (BASE[1], BASE[3]), numbers, arrived)
    for copy in copies:
        copy.start()
    acc[...] = first[...]
    edge[...] = first_edge[...]
    total[...] = (w0[...] + w2[...]) + (n1[:W_ROWS, :] + n3[:W_ROWS, :])
    for copy in copies:
        copy.wait()
    add_frames((n1, n3), (BASE[1], BASE[3]), acc, edge, numbers)

    def pack(out, group):
        for n, shift in enumerate(group):
            to = lax.rem(z + shift, NZ)
            start = n * Z_ROWS
            for k in range(OWN):
                at = start + k * 3 * GROUP
                out[at : at + 3 * GROUP, :] = acc[OWN * to + k]
                at = start + OWN * 3 * GROUP + 3 * k
                out[at : at + 3, :] = edge[OWN * to + k, 0:3, :]
            at = start + OWN * (3 * GROUP + 3)
            for c in range(3):
                for j in range(2):
                    row = pl.ds(GROUP * c + 2 * to + j, 1)
                    out[at + 2 * c + j : at + 2 * c + j + 1, :] = total[row, :]
            row = slice(3 * GROUP, 3 * GROUP + 3)
            out[at + 6 : at + 9, :] = total[row, :]
            out[at + 9 : start + Z_ROWS, :] = jnp.zeros((Z_ROWS - OWN * (3 * GROUP + 3) - 9, SIZE), F32)

    pack(keep, KEEP)
    pack(up, UP[:2])
    pack(down, DOWN[:2])
    pack(block, UP[2:])
    up[2 * Z_ROWS :, :] = block[:Z_FIRST, :]
    down[2 * Z_ROWS :, :] = block[Z_FIRST:, :]


def relay_kernel(keep, up, down, far, back):
    end = 2 * Z_ROWS
    far[:Z_FIRST, :] = keep[Z_ROWS : Z_ROWS + Z_FIRST, :] + (up[end:, :] + down[Z_ROWS : Z_ROWS + Z_FIRST, :])
    far[Z_FIRST:, :] = keep[Z_ROWS + Z_FIRST : end, :] + down[Z_ROWS + Z_FIRST : end, :]
    back[:Z_FIRST, :] = keep[end : end + Z_FIRST, :] + up[Z_ROWS : Z_ROWS + Z_FIRST, :]
    back[Z_FIRST:, :] = keep[end + Z_FIRST :, :] + (up[Z_ROWS + Z_FIRST : end, :] + down[end:, :])


def quotient(num_re, num_im, den):
    den = PRIOR_WEIGHT + den
    return num_re / den, num_im / den


def object_kernel(keep, up, down, far, back, out):
    own = slice(0, Z_ROWS)
    sums = (keep[own, :] + (up[own, :] + down[own, :])) + (far[...] + back[...])
    for k in range(OWN):
        base = k * 3 * GROUP
        re, im = quotient(*(sums[base + c * GROUP : base + (c + 1) * GROUP] for c in range(3)))
        out[k * 2 * GROUP : k * 2 * GROUP + GROUP, :] = re
        out[k * 2 * GROUP + GROUP : (k + 1) * 2 * GROUP, :] = im
        base = OWN * 3 * GROUP + 3 * k
        re, im = quotient(*(sums[base + c : base + c + 1] for c in range(3)))
        at = OWN * 2 * GROUP + 2 * k
        out[at : at + 1, :] = re
        out[at + 1 : at + 2, :] = im
    base = OWN * (3 * GROUP + 3)
    at = OWN * (2 * GROUP + 2)
    re, im = quotient(*(sums[base + 2 * c : base + 2 * c + 2] for c in range(3)))
    out[at : at + 2, :] = re
    out[at + 2 : at + 4, :] = im
    re, im = quotient(*(sums[base + 6 + c : base + 7 + c] for c in range(3)))
    out[at + 4 : at + 5, :] = re
    out[at + 5 : at + 6, :] = im
    out[at + 6 :, :] = jnp.zeros((F_ROWS - at - 6, SIZE), F32)


def select_kernel(place, ids, own, ahead, behind, up, down, *refs):
    outs, wides, (near, objects, edge, total, other) = refs[:NY], refs[NY : 2 * NY], refs[2 * NY :]
    other[:F_FIRST, :] = up[2 * F_ROWS :, :]
    other[F_FIRST:, :] = down[2 * F_ROWS :, :]
    y, z = place[0], place[1]
    parts = ((0, own, 0), (3, ahead, 0), (5, behind, 0), (7, up, 0), (2, up, 1), (1, down, 0), (6, down, 1), (4, other, 0))
    for shift, part, n in parts:
        source = lax.rem(z + shift, NZ)
        start = n * F_ROWS
        for k in range(OWN):
            at = start + k * 2 * GROUP
            objects[OWN * source + k] = part[at : at + 2 * GROUP, :]
            at = start + OWN * 2 * GROUP + 2 * k
            edge[OWN * source + k, 0:2, :] = part[at : at + 2, :]
        at = start + OWN * (2 * GROUP + 2)
        for j in range(2):
            total[pl.ds(2 * source + j, 1), :] = part[at + j : at + j + 1, :]
            total[pl.ds(GROUP + 2 * source + j, 1), :] = part[at + 2 + j : at + 3 + j, :]
    for shift in range(NY):
        out = outs[shift]
        start = (NY - shift) % NY * FRAMES
        for f in range(FRAMES):
            out[f * 2 * GROUP : (f + 1) * 2 * GROUP, :] = objects[ids[start + f]]
        wides[shift][: 2 * GROUP, :] = objects[lax.rem(y + shift, NY) * NZ + z]
        wides[shift][2 * GROUP :, :] = total[...]
    for f in range(FRAMES):
        near[2 * f : 2 * f + 2, :] = edge[ids[f], 0:2, :]
    near[2 * FRAMES : 2 * FRAMES + 2, :] = edge[y * NZ + z, 0:2, :]
    at = OWN * (2 * GROUP + 2) + 4
    near[2 * FRAMES + 2 : 2 * FRAMES + 4, :] = own[at : at + 2, :]
    near[2 * FRAMES + 4 :, :] = jnp.zeros((4, SIZE), F32)


def plain(kernel, name, smems, arrays, outs, scratch, cost=None):
    return pl.pallas_call(
        kernel,
        in_specs=[smem()] * len(smems) + [pl.BlockSpec(memory_space=pltpu.VMEM)] * len(arrays),
        out_specs=[pl.BlockSpec(memory_space=pltpu.VMEM)] * len(outs),
        out_shape=outs,
        scratch_shapes=scratch,
        compiler_params=pltpu.CompilerParams(vmem_limit_bytes=VMEM_SMALL),
        cost_estimate=cost,
        name=name,
    )(*smems, *arrays)


def backward_kernel(wide, place, q_ref, s_ref, d_ref, g_ref, *refs):
    parts, refs = refs[:NY], refs[NY:]
    if not wide:
        other, *refs = refs
    near, a1, a2, b1, b2, e1, e2, f1, f2, m1, m2, out, *objs, scr = refs
    step = pl.program_id(0)
    y = place[0]

    def gather(sources, at):
        for shift in range(NY):
            row = pl.multiple_of(GROUP * lax.rem(y + NY - shift, NY), GROUP)
            for c in range(2):
                scr[c, pl.ds(row, GROUP), :] = sources[shift][at + c * GROUP : at + (c + 1) * GROUP, :]

    @pl.when(step == 0)
    def _():
        scr[...] = jnp.zeros_like(scr)
        for item, obj in enumerate(objs):
            gather(parts, item * 2 * GROUP)
            at = 2 * (FRAMES + item)
            for c in range(2):
                scr[c, 64:65, :] = near[at + c : at + c + 1, :]
            half = jnp.concatenate([scr[0, :64, :], scr[1, :64, :]], 0)
            high = half.astype(BF16)
            middle, low = cut(half - high.astype(F32))
            turned = jnp.zeros((SIZE, SIZE), F32)
            for part in (high, middle, low):
                turned = turned + mm(m1[...], mm(part, m2[...]).astype(BF16))
            for c in range(2):
                obj[c, :64, :] = scr[c, :64, :]
                obj[c, 64:, :] = turned[64 * c : 64 * (c + 1)]
                obj[c, 64:65, :] = scr[c, 64:65, :]

    cots = []
    for k in range(STEP):
        if not wide:
            gather(parts, k * 2 * GROUP)
            for c in range(2):
                scr[c, 64:65, :] = near[pl.ds(2 * (step * STEP + k) + c, 1), :]
        fr, fi = scr[0], scr[1]
        sk, dk = s_ref[k], d_ref[k]
        sr, si, dr, di = sk[:, :SIZE], sk[:, SIZE:], dk[:, :SIZE], dk[:, SIZE:]
        rest_r = dr - (fr * sr - fi * si)
        rest_i = di - (fr * si + fi * sr)
        cots.append(jnp.concatenate([-(rest_r * fr + rest_i * fi), rest_r * fi - rest_i * fr], 1))
    t = right_mul(jnp.concatenate(cots, 0), a1, a2)
    steps = []
    for a in range(0, STEP, 2):
        cols = []
        for k in (a, a + 1):
            tk = t[k * ROWS : (k + 1) * ROWS]
            cols.append(jnp.concatenate([tk[:, :SIZE], tk[:, SIZE:]], 0))
        dp = left_mul(b1, b2, jnp.concatenate(cols, 1))
        fields = []
        for k in (a, a + 1):
            gr, gi = g_ref[k, 0], g_ref[k, 1]
            power = gr * gr + gi * gi
            scale = 1.0 / jnp.sum(power, keepdims=True)
            dk = dp[:, (k - a) * SIZE : (k - a + 1) * SIZE]
            mean = jnp.sum(dk * power, keepdims=True) * scale
            dk = (dk - mean) * (scale * (4.0 / (SIZE * SIZE)))
            fields.append(jnp.concatenate([gr * dk, gi * dk], 0))
        h = left_mul(e1, e2, jnp.concatenate(fields, 1))
        for k in (a, a + 1):
            lanes = slice((k - a) * SIZE, (k - a + 1) * SIZE)
            steps.append(jnp.concatenate([h[:PUP, lanes], h[PUP:, lanes]], 1))
    dq = right_mul(jnp.concatenate(steps, 0), f1, f2)
    low = low_lanes(PUP // 2)
    flat = []
    for k in range(STEP):
        m = q_ref[k] * pltpu.roll(dq[k * PUP : (k + 1) * PUP], PUP, 1)
        m = m - pltpu.roll(m, PUP, 1)
        dphase = jnp.where(low, m[: PUP // 2], -m[PUP // 2 :])
        if wide:
            out[k] = dphase
        else:
            flat.append(dphase + other[k])
    for at in range(0, FRAMES if flat else 0, STEP):

        @pl.when(step * STEP == at)
        def _(at=at):
            for k, dphase in enumerate(flat):
                for r in range(PUP // 2):
                    out[at + k : at + k + 1, r * SIZE : (r + 1) * SIZE] = dphase[r : r + 1]


def backward(wide, place, q, s, d, g, parts, near, other, tables):
    block = 2 * GROUP
    pairs = pl.BlockSpec((STEP, PUP // 2, SIZE), lambda i: (i, 0, 0))
    if wide:
        sources, specs = list(parts), [whole(p) for p in parts]
        dphase, dphase_spec = shape(FRAMES, PUP // 2, SIZE), pairs
    else:
        sources = list(parts) + [other]
        specs = [pl.BlockSpec((STEP * block, SIZE), lambda i: (i, 0))] * NY
        specs += [pairs]
        dphase = shape(FRAMES, PUP * PUP)
        dphase_spec = pl.BlockSpec(dphase.shape, lambda i: (0, 0))
    return pl.pallas_call(
        functools.partial(backward_kernel, wide),
        grid=(FRAMES // STEP,),
        in_specs=[
            smem(),
            pl.BlockSpec((STEP, PUP, 2 * PUP), lambda i: (i, 0, 0)),
            pl.BlockSpec((STEP, ROWS, 2 * SIZE), lambda i: (i, 0, 0)),
            pl.BlockSpec((STEP, ROWS, 2 * SIZE), lambda i: (i, 0, 0)),
            pl.BlockSpec((STEP, 2, SIZE, SIZE), lambda i: (i, 0, 0, 0)),
        ]
        + specs
        + [whole(near)]
        + [whole(t) for t in tables],
        out_specs=[dphase_spec] + [pl.BlockSpec((2, SIZE, SIZE), lambda i: (0, 0, 0))] * (2 * wide),
        out_shape=[dphase] + [shape(2, SIZE, SIZE)] * (2 * wide),
        scratch_shapes=[pltpu.VMEM((2, ROWS, SIZE), F32)],
        compiler_params=pltpu.CompilerParams(vmem_limit_bytes=VMEM_LIMIT),
        cost_estimate=pl.CostEstimate(flops=4_000_000_000, bytes_accessed=8_000_000, transcendentals=0),
        name="backward_wide" if wide else "backward_narrow",
    )(place, q, s, d, g, *sources, near, *tables)


def along(axis, shift):
    pairs = []
    for y in range(NY):
        for z in range(NZ):
            to = ((y + shift) % NY, z) if axis == "y" else (y, (z + shift) % NZ)
            pairs.append((y * NZ + z, to[0] * NZ + to[1]))
    return pairs


def send(x, axis, shift):
    return lax.ppermute(x, "chan", along(axis, shift))


def shards(alpha, images, modes, diversity, chan_of_frame):
    tables_f, tables_b = ([jnp.asarray(t) for t in group] for group in make_tables())
    here = lax.axis_index("chan")
    place = jnp.stack([here // NZ, here % NZ]).astype(jnp.int32)
    own_ids = jnp.zeros((8, SIZE), F32).at[0, :FRAMES].set(chan_of_frame[:, 0].astype(F32))

    phase = jnp.dot(alpha, modes, precision=lax.Precision.HIGH).reshape(FRAMES, PUP // 2, SIZE)
    axis = np.arange(PUP, dtype=np.float32) - (PUP - 1) / 2.0
    pupil = (axis[:, None] ** 2 + axis[None, :] ** 2 <= (PUP / 2.0) ** 2).astype(np.float32)
    pupil = jnp.asarray(pupil.reshape(PUP // 2, SIZE))
    extra = [diversity.reshape(PUP // 2, SIZE), own_ids]

    *narrow_kept, n0, n1, n2, n3 = forward(False, place, phase, pupil, extra, images[:, 1:], tables_f)
    *wide_kept, w0, n1, w2, n3 = forward(True, place, phase, pupil, [n1, n3], images, tables_f)
    n2 = send(n2, "y", 2)
    reading = [pltpu.SMEM((2, 8, SIZE), F32), pltpu.SemaphoreType.DMA((2,))]
    first, first_edge = plain(
        first_sum_kernel,
        "sum_first",
        [],
        [n0, n2],
        [shape(32, 3 * GROUP, SIZE), shape(32, 8, SIZE)],
        reading,
        pl.CostEstimate(flops=4_000_000_000, bytes_accessed=2_000_000, transcendentals=0),
    )
    n1, n3 = send(n1, "y", 1), send(n3, "y", 3)
    keep, up, down = plain(
        sum_kernel,
        "sum_channels",
        [place],
        [first, first_edge, n1, n3, w0, send(w2, "y", 2)],
        [shape(rows, SIZE) for rows in (3 * Z_ROWS, UP_ROWS, DOWN_ROWS)],
        [
            pltpu.VMEM((32, 3 * GROUP, SIZE), F32),
            pltpu.VMEM((32, 8, SIZE), F32),
            pltpu.VMEM((Z_ROWS, SIZE), F32),
            pltpu.VMEM((W_ROWS, SIZE), F32),
            *reading,
        ],
    )
    ids = jnp.concatenate([n[base + IDS, :FRAMES] for n, base in zip((n0, n1, n2, n3), BASE, strict=True)])
    ids = ids.astype(jnp.int32)
    up, down = send(up, "z", 1), send(down, "z", -1)
    far, back = plain(relay_kernel, "relay", [], [keep, up, down], [shape(Z_ROWS, SIZE)] * 2, [])
    far, back = send(far, "z", 3), send(back, "z", -3)
    (own,) = plain(object_kernel, "objects", [], [keep, up, down, far, back], [shape(F_ROWS, SIZE)], [])
    ahead, behind = send(own, "z", -3), send(own, "z", 3)
    up = send(jnp.concatenate([own, ahead, behind[:F_FIRST]]), "z", 1)
    down = send(jnp.concatenate([own, behind, ahead[F_FIRST:]]), "z", -1)
    *back, near = plain(
        select_kernel,
        "select_objects",
        [place, ids],
        [own, ahead, behind, up, down],
        [shape(R_ROWS, SIZE)] * NY + [shape(4 * GROUP, SIZE)] * NY + [shape(2 * FRAMES + 8, SIZE)],
        [pltpu.VMEM((32, 2 * GROUP, SIZE), F32), pltpu.VMEM((32, 8, SIZE), F32), pltpu.VMEM((2 * GROUP, SIZE), F32), pltpu.VMEM((F_ROWS, SIZE), F32)],
    )
    back, wide_back = back[:NY], back[NY:]
    wide_back = [wide_back[0]] + [send(wide_back[k], "y", k) for k in range(1, NY)]
    back = [back[0]] + [send(back[k], "y", k) for k in range(1, NY)]

    wide_dphase, narrow_object, wide_object = backward(True, place, *wide_kept, wide_back, near, None, tables_b)
    (dphase,) = backward(False, place, *narrow_kept, back, near, wide_dphase, tables_b)
    gradient = lax.dot_general(dphase, modes, (((1,), (1,)), ((), ())), precision=lax.Precision.HIGH)
    return gradient, narrow_object[None], wide_object


def solution(mesh):
    placed = (
        P(("patch", "chan"), None),
        P(("patch", "chan"), None, None, None),
        P(),
        P(),
        P("chan", None),
    )
    return jax.shard_map(
        shards,
        mesh=mesh,
        in_specs=placed,
        out_specs=(
            P(("patch", "chan"), None),
            P(("patch", "chan"), None, None, None),
            P("patch", None, None),
        ),
        check_vma=False,
    )
```
